32 devices in a mesh: vintage: 4 (over y, core), inline: 4 (over z), xline: 2 (over x).
Axes of the slice: x: 2, y: 2, z: 4, core: 2. Of those that a mesh axis runs over, the one named last changes fastest.
Arguments:
- amplitude: float32 [4, 32, 32, 256], P('vintage', 'inline', 'xline'), may hold values from -6 to 6
- inline_slope: int32 [4, 32, 32], P('vintage', 'inline', 'xline'), may hold values from -2 to 2
- crossline_slope: int32 [4, 32, 32], P('vintage', 'inline', 'xline'), may hold values from -2 to 2
Outputs:
- semblance: float32 [4, 32, 32, 256], P('vintage', 'inline', 'xline')
- lag_correl: float32 [4, 32, 32, 264], P('vintage', 'inline', 'xline')
The draws below stay inside these ranges and needn't reach their ends.
All inputs are finite; a program needn't handle non-finite values.
Results may differ from the reference program's by a relative error of at most 0.0003.
Values sent between devices are 32-bit elements; how exact they have to be, the bound alone decides.
A program may use at most 64 MiB of HBM per device.

```python
import jax
import jax.numpy as jnp
from jax import lax

TIME_SAMPLES = 256
MAX_DIP_STEP = 2
RT = 4
LAGS = 33
NWIN = 8
SURVEY_COUNT = 4
INLINE_TRACES = 32
CROSSLINE_COUNT = 32


def touch_ends(drawn, own_key, smallest, high):
    place = [jax.random.randint(jax.random.fold_in(own_key, axis), (), 0, length) for axis, length in enumerate(drawn.shape)]
    longest = drawn.shape.index(max(drawn.shape))
    beside = place[:longest] + [(place[longest] + 1) % drawn.shape[longest]] + place[longest + 1:]
    return drawn.at[tuple(place)].set(smallest).at[tuple(beside)].set(high)


def block_scale(own_key, shape, split, least, largest):
    def one(dim, shards_of):
        steps = jax.random.uniform(jax.random.fold_in(jax.random.fold_in(own_key, 6), dim), (shards_of,), jnp.float32, least / len(split), largest / len(split))
        return jnp.repeat(jnp.exp(steps), shape[dim] // shards_of).reshape((-1,) + (1,) * (len(shape) - dim - 1))

    level = one(*split[0])
    for cut in split[1:]:
        level = level * one(*cut)
    return level


def centred(rng, shape, width, most, shards=(), kind=jnp.bfloat16):
    array = jax.random.normal(rng, shape, jnp.float32) * width
    if len(shards) > 0:
        array = block_scale(rng, shape, shards, -0.22, 0.18) * array
    return jnp.clip(array, min=-most, max=most).astype(kind)


def setup_inputs(seed: int = 0) -> dict:
    key_of = jax.random.split(jax.random.key(seed), 4)
    return {
        "amplitude": centred(key_of[0], (SURVEY_COUNT, INLINE_TRACES, CROSSLINE_COUNT, TIME_SAMPLES), 1.0, 6.0, ((0, 4), (1, 4), (2, 2)), jnp.float32),
        "inline_slope": touch_ends(jax.random.randint(key_of[1], (SURVEY_COUNT, INLINE_TRACES, CROSSLINE_COUNT), 0 - MAX_DIP_STEP, MAX_DIP_STEP + 1), jax.random.fold_in(key_of[1], 1), 0 - MAX_DIP_STEP, MAX_DIP_STEP).astype(jnp.int32),
        "crossline_slope": touch_ends(jax.random.randint(key_of[2], (SURVEY_COUNT, INLINE_TRACES, CROSSLINE_COUNT), 0 - MAX_DIP_STEP, MAX_DIP_STEP + 1), jax.random.fold_in(key_of[2], 1), 0 - MAX_DIP_STEP, MAX_DIP_STEP).astype(jnp.int32),
    }


EPS = 1e-06

def attribute_padded(padded, dip_il, dip_xl):
    inner_i = padded.shape[0] - 2
    inner_x = padded.shape[1] - 2
    padding = 2 * MAX_DIP_STEP + RT
    extent = TIME_SAMPLES + 2 * RT
    stack = jnp.zeros((inner_i, inner_x, extent), jnp.float32)
    power = jnp.zeros((inner_i, inner_x, extent), jnp.float32)
    for row_step in (-1, 0, 1):
        for col_step in (-1, 0, 1):
            neighbor = padded[1 + row_step:1 + row_step + inner_i, 1 + col_step:1 + col_step + inner_x, :]
            shift_map = row_step * dip_il + col_step * dip_xl
            reach = (abs(row_step) + abs(col_step)) * MAX_DIP_STEP
            moved = jnp.zeros((inner_i, inner_x, extent), jnp.float32)
            for offset_value in range(-reach, reach + 1):
                start = padding - RT + offset_value
                shifted = neighbor[:, :, start:start + extent]
                moved = jnp.where((shift_map == offset_value)[:, :, None], shifted, moved)
            stack = stack + moved
            power = power + moved * moved
    numer = jnp.zeros((inner_i, inner_x, TIME_SAMPLES), jnp.float32)
    denom = jnp.zeros((inner_i, inner_x, TIME_SAMPLES), jnp.float32)
    for window_step in range(2 * RT + 1):
        piece = stack[:, :, window_step:window_step + TIME_SAMPLES]
        numer = numer + piece * piece
        denom = denom + power[:, :, window_step:window_step + TIME_SAMPLES]
    semb = numer / (9.0 * denom + EPS)
    attr = semb * stack[:, :, RT:RT + TIME_SAMPLES] / 9.0
    return (semb, attr)

def attribute(volume, dip_il, dip_xl):
    padding = 2 * MAX_DIP_STEP + RT
    padded = jnp.pad(volume, ((1, 1), (1, 1), (padding, padding)))
    return attribute_padded(padded, dip_il, dip_xl)

def correlate(monitor, baseline):
    half_lags = LAGS // 2
    inner_i, inner_x = (monitor.shape[0], monitor.shape[1])
    base_pad = jnp.pad(baseline, ((0, 0), (0, 0), (half_lags, half_lags)))
    mon_energy = lax.optimization_barrier(jnp.sum(monitor * monitor, axis=-1))
    base_energy = lax.optimization_barrier(jnp.sum(baseline * baseline, axis=-1))
    factor = NWIN / jnp.sqrt(mon_energy * base_energy + EPS)
    columns = []
    for lag_index in range(LAGS):
        product = monitor * base_pad[:, :, lag_index:lag_index + TIME_SAMPLES]
        columns.append(lax.optimization_barrier(jnp.sum(product.reshape(inner_i, inner_x, NWIN, TIME_SAMPLES // NWIN), axis=-1)))
    result = jnp.stack(columns, axis=2) * factor[:, :, None, None]
    return result.reshape(inner_i, inner_x, LAGS * NWIN)

def reference(amplitude, inline_slope, crossline_slope):
    _, base_attr = attribute(amplitude[0], inline_slope[0], crossline_slope[0])

    def one_vintage(items):
        semb, attr = attribute(items[0], items[1], items[2])
        return (semb, correlate(attr, base_attr))
    semb_all, correl_all = lax.map(one_vintage, (amplitude, inline_slope, crossline_slope))
    return (semb_all, correl_all)
```

```python
import functools

import jax
import jax.numpy as jnp
from jax import lax
from jax.experimental import pallas as pl
from jax.experimental.pallas import tpu as pltpu
from jax.sharding import PartitionSpec as P

TIME_SAMPLES = 256
MAX_DIP_STEP = 2
RT = 4
LAGS = 33
NWIN = 8
EPS = 1e-06

WIN = TIME_SAMPLES // NWIN
HALF = LAGS // 2
REACH = 2 * MAX_DIP_STEP
PAD = 8
CHUNK = 8
CHUNKS = WIN // CHUNK
MESH = pl.DeviceIdType.MESH
DIRECTIONS = [(a, b) for a in (-1, 0, 1) for b in (-1, 0, 1) if (a, b) != (0, 0)]
OFFSETS = [(a, b) for a in (-1, 0, 1) for b in (-1, 0, 1)]


def lane_dips(dips, rows, cols):
    lanes = rows * cols
    col = lax.broadcasted_iota(jnp.int32, (cols, lanes), 0)
    lane = lax.broadcasted_iota(jnp.int32, (cols, lanes), 1)
    spread = jnp.where(lane % cols == col, 1.0, 0.0).astype(jnp.float32)
    tiled = jnp.dot(dips.astype(jnp.float32), spread, preferred_element_type=jnp.float32)
    row = lax.broadcasted_iota(jnp.int32, (rows, lanes), 0)
    here = lax.broadcasted_iota(jnp.int32, (rows, lanes), 1) // cols == row
    return jnp.sum(jnp.where(here, tiled, 0.0), axis=0, keepdims=True)


def select_shift(rows, shift, reach):
    left = shift + float(reach)
    step = 8 if reach > 3 else 4
    while step:
        on = left >= float(step)
        left = jnp.where(on, left - float(step), left)
        count = len(rows) - step if step > 1 else CHUNK
        keep = min(count, len(rows))
        need = CHUNK + step - 1
        rows = [
            jnp.where(on, rows[k + step], rows[k]) if k + step < len(rows) else rows[k]
            for k in range(min(len(rows), need))
        ]
        step //= 2
    return rows[:CHUNK]


def kernel(
    rows, cols, vintages, inlines, xlines,
    amp, dip_il, dip_xl, semb_out, corr_out,
    tile, times, stack, power, attr, base, semb_t, semb_n, corr_t, corr_n, d_il, d_xl,
    load_sem, store_sem, halo_send, halo_recv, base_send, base_recv,
):
    v = lax.axis_index("vintage")
    i = lax.axis_index("inline")
    x = lax.axis_index("xline")
    loads = [
        pltpu.make_async_copy(amp.at[0], tile.at[pl.ds(1, rows), pl.ds(PAD, cols), :], load_sem.at[0]),
        pltpu.make_async_copy(dip_il.at[0], d_il, load_sem.at[1]),
        pltpu.make_async_copy(dip_xl.at[0], d_xl, load_sem.at[2]),
    ]
    for load in loads:
        load.start()

    edge = jnp.zeros((PAD, TIME_SAMPLES), jnp.float32)
    for row in range(rows + 2):
        tile[row, 0:PAD, :] = edge
        tile[row, PAD + cols : 2 * PAD + cols, :] = edge
    for row in (0, rows + 1):
        tile[row, PAD : PAD + cols, :] = jnp.zeros((cols, TIME_SAMPLES), jnp.float32)

    def inside(a, b):
        return (i + a >= 0) & (i + a < inlines) & (x + b >= 0) & (x + b < xlines)

    barrier = pltpu.get_barrier_semaphore()
    greeted = jnp.int32(0)
    for a, b in DIRECTIONS:
        there = inside(a, b)
        greeted = greeted + jnp.where(there, 1, 0)

        @pl.when(there)
        def _():
            pl.semaphore_signal(
                barrier, inc=1, device_id={"inline": i + a, "xline": x + b}, device_id_type=MESH
            )

    @pl.when(v != 0)
    def _():
        pl.semaphore_signal(barrier, inc=1, device_id={"vintage": 0}, device_id_type=MESH)

    greeted = greeted + jnp.where(v == 0, vintages - 1, 0)
    pl.semaphore_wait(barrier, greeted)

    def halo(index):
        a, b = DIRECTIONS[index]
        row_from = {-1: pl.ds(0, 1), 0: pl.ds(0, rows), 1: pl.ds(rows - 1, 1)}[a]
        row_to = {-1: pl.ds(rows + 1, 1), 0: pl.ds(1, rows), 1: pl.ds(0, 1)}[a]
        col_from = {-1: pl.ds(0, PAD), 0: pl.ds(0, cols), 1: pl.ds(cols - PAD, PAD)}[b]
        col_to = {-1: pl.ds(PAD + cols, PAD), 0: pl.ds(PAD, cols), 1: pl.ds(0, PAD)}[b]
        return pltpu.make_async_remote_copy(
            src_ref=amp.at[0, row_from, col_from, :],
            dst_ref=tile.at[row_to, col_to, :],
            send_sem=halo_send.at[index],
            recv_sem=halo_recv.at[index],
            device_id={"inline": i + a, "xline": x + b},
            device_id_type=MESH,
        )

    for index, (a, b) in enumerate(DIRECTIONS):

        @pl.when(inside(a, b))
        def _():
            halo(index).start()

    for load in loads:
        load.wait()
    dips = [lane_dips(d_il[...], rows, cols), lane_dips(d_xl[...], rows, cols)]
    lanes = rows * cols
    dips = [jnp.broadcast_to(dip, (NWIN, lanes)) for dip in dips]
    blank = jnp.zeros((PAD, lanes), jnp.float32)
    for slot in range(len(OFFSETS)):
        times[slot, 0:PAD, :] = blank
        times[slot, PAD + TIME_SAMPLES : 2 * PAD + TIME_SAMPLES, :] = blank

    for index, (a, b) in enumerate(DIRECTIONS):

        @pl.when(inside(-a, -b))
        def _():
            halo(index).wait_recv()

    for slot, (a, b) in enumerate(OFFSETS):
        block = tile[1 + a : 1 + a + rows, PAD + b : PAD + b + cols, :]
        times[slot, PAD : PAD + TIME_SAMPLES, :] = block.reshape(lanes, TIME_SAMPLES).T

    @pl.loop(0, CHUNKS + 1)
    def _(chunk):
        first = chunk * CHUNK
        total = [None] * CHUNK
        squares = [None] * CHUNK
        for slot, (a, b) in enumerate(OFFSETS):
            reach = (abs(a) + abs(b)) * MAX_DIP_STEP
            taps = [
                times[slot, pl.ds(first + REACH - reach + k, NWIN, stride=WIN), :]
                for k in range(CHUNK + 2 * reach)
            ]
            moved = taps
            if reach:
                moved = select_shift(taps, float(a) * dips[0] + float(b) * dips[1], reach)
            for k in range(CHUNK):
                square = moved[k] * moved[k]
                total[k] = moved[k] if total[k] is None else total[k] + moved[k]
                squares[k] = square if squares[k] is None else squares[k] + square
        for k in range(CHUNK):
            stack[first + k] = total[k]
            power[first + k] = squares[k]

    def window(values):
        twos = [values[k] + values[k + 1] for k in range(len(values) - 1)]
        fours = [twos[k] + twos[k + 2] for k in range(len(twos) - 2)]
        return [fours[k] + fours[k + 4] + values[k + 8] for k in range(CHUNK)]

    def share(chunk, other):
        return pltpu.make_async_remote_copy(
            src_ref=attr.at[pl.ds(chunk * CHUNK, CHUNK)],
            dst_ref=base.at[pl.ds(HALF + chunk * CHUNK, CHUNK)],
            send_sem=base_send.at[chunk, other - 1],
            recv_sem=base_recv.at[chunk],
            device_id={"vintage": other},
            device_id_type=MESH,
        )

    @pl.loop(0, CHUNKS)
    def _(chunk):
        first = chunk * CHUNK
        sums = [stack[first + k] for k in range(CHUNK + 2 * RT)]
        numer = window([s * s for s in sums])
        denom = window([power[first + k] for k in range(CHUNK + 2 * RT)])
        for k in range(CHUNK):
            semb = numer[k] / (9.0 * denom[k] + EPS)
            semb_t[pl.ds(first + k, NWIN, stride=WIN), :] = semb
            attr[first + k] = semb * sums[RT + k] * (1.0 / 9.0)

        @pl.when(v == 0)
        def _():
            for other in range(1, vintages):
                share(chunk, other).start()

    semb_n[...] = semb_t[...].T
    semb_store = pltpu.make_async_copy(semb_n, semb_out, store_sem.at[0])
    semb_store.start()

    def energy(ref, first):
        parts = [ref[first + k] * ref[first + k] for k in range(WIN)]
        while len(parts) > 1:
            parts = [parts[k] + parts[k + 1] for k in range(0, len(parts), 2)]
        return jnp.sum(parts[0], axis=0, keepdims=True)

    mon_energy = energy(attr, 0)

    @pl.when(v == 0)
    def _():
        base[HALF : HALF + WIN] = attr[...]

    @pl.when(v != 0)
    def _():
        for chunk in range(CHUNKS):
            share(chunk, 1).wait_recv()

    base_energy = energy(base, HALF)
    win = lax.broadcasted_iota(jnp.int32, (NWIN, lanes), 0)
    for k in range(HALF):
        base[k] = jnp.where(win == 0, 0.0, pltpu.roll(base[k + WIN], 1, 0))
        base[k + HALF + WIN] = jnp.where(win == NWIN - 1, 0.0, pltpu.roll(base[k + HALF], NWIN - 1, 0))

    def add_chunk(chunk, acc):
        first = chunk * CHUNK
        mine = [attr[first + k] for k in range(CHUNK)]
        acc = list(acc)
        for j in range(CHUNK + LAGS - 1):
            other = base[first + j]
            for k in range(CHUNK):
                if 0 <= j - k < LAGS:
                    acc[j - k] = acc[j - k] + mine[k] * other
        return tuple(acc)

    zero = jnp.zeros((NWIN, lanes), jnp.float32)
    acc = lax.fori_loop(0, CHUNKS, add_chunk, (zero,) * LAGS)
    factor = jnp.broadcast_to(NWIN / jnp.sqrt(mon_energy * base_energy + EPS), (NWIN, lanes))
    for lag in range(LAGS):
        corr_t[lag * NWIN : (lag + 1) * NWIN, :] = acc[lag] * factor
    corr_n[:, 0:TIME_SAMPLES] = corr_t[0:TIME_SAMPLES, :].T
    corr_n[:, TIME_SAMPLES : LAGS * NWIN] = corr_t[TIME_SAMPLES : LAGS * NWIN, :].T
    corr_store = pltpu.make_async_copy(corr_n, corr_out, store_sem.at[1])
    corr_store.start()

    for index, (a, b) in enumerate(DIRECTIONS):

        @pl.when(inside(a, b))
        def _():
            halo(index).wait_send()

    @pl.when(v == 0)
    def _():
        for chunk in range(CHUNKS):
            for other in range(1, vintages):
                share(chunk, other).wait_send()

    semb_store.wait()
    corr_store.wait()


def per_device(vintages, inlines, xlines, amplitude, inline_slope, crossline_slope):
    _, rows, cols, _ = amplitude.shape
    lanes = rows * cols
    f32 = jnp.float32
    anywhere = pl.BlockSpec(memory_space=pl.ANY)
    semb, correl = pl.pallas_call(
        functools.partial(kernel, rows, cols, vintages, inlines, xlines),
        out_shape=(
            jax.ShapeDtypeStruct((lanes, TIME_SAMPLES), f32),
            jax.ShapeDtypeStruct((lanes, LAGS * NWIN), f32),
        ),
        in_specs=[anywhere] * 3,
        out_specs=(anywhere, anywhere),
        scratch_shapes=[
            pltpu.VMEM((rows + 2, cols + 2 * PAD, TIME_SAMPLES), f32),
            pltpu.VMEM((len(OFFSETS), TIME_SAMPLES + 2 * PAD, lanes), f32),
            pltpu.VMEM((WIN + 2 * RT, NWIN, lanes), f32),
            pltpu.VMEM((WIN + 2 * RT, NWIN, lanes), f32),
            pltpu.VMEM((WIN, NWIN, lanes), f32),
            pltpu.VMEM((WIN + 2 * HALF, NWIN, lanes), f32),
            pltpu.VMEM((TIME_SAMPLES, lanes), f32),
            pltpu.VMEM((lanes, TIME_SAMPLES), f32),
            pltpu.VMEM((LAGS * NWIN, lanes), f32),
            pltpu.VMEM((lanes, LAGS * NWIN), f32),
            pltpu.VMEM((rows, cols), jnp.int32),
            pltpu.VMEM((rows, cols), jnp.int32),
            pltpu.SemaphoreType.DMA((3,)),
            pltpu.SemaphoreType.DMA((2,)),
            pltpu.SemaphoreType.DMA((len(DIRECTIONS),)),
            pltpu.SemaphoreType.DMA((len(DIRECTIONS),)),
            pltpu.SemaphoreType.DMA((CHUNKS, max(vintages - 1, 1))),
            pltpu.SemaphoreType.DMA((CHUNKS,)),
        ],
        compiler_params=pltpu.CompilerParams(
            collective_id=0, has_side_effects=True, vmem_limit_bytes=16 * 2**20
        ),
        name="steer_and_correlate",
    )(amplitude, inline_slope, crossline_slope)
    return (
        semb.reshape(1, rows, cols, TIME_SAMPLES),
        correl.reshape(1, rows, cols, LAGS * NWIN),
    )


def solution(mesh):
    sizes = [mesh.shape[axis] for axis in ("vintage", "inline", "xline")]
    return jax.shard_map(
        functools.partial(per_device, *sizes),
        mesh=mesh,
        in_specs=(
            P("vintage", "inline", "xline", None),
            P("vintage", "inline", "xline"),
            P("vintage", "inline", "xline"),
        ),
        out_specs=(P("vintage", "inline", "xline", None), P("vintage", "inline", "xline", None)),
        check_vma=False,
    )
```

```python
import functools

import jax
import jax.numpy as jnp
from jax import lax
from jax.experimental import pallas as pl
from jax.experimental.pallas import tpu as pltpu
from jax.sharding import PartitionSpec as P

TIME_SAMPLES = 256
MAX_DIP_STEP = 2
RT = 4
LAGS = 33
NWIN = 8
EPS = 1e-06

WIN = TIME_SAMPLES // NWIN
HALF = LAGS // 2
REACH = 2 * MAX_DIP_STEP
PAD = 8
CHUNK = 8
CHUNKS = WIN // CHUNK
MESH = pl.DeviceIdType.MESH
DIRECTIONS = [(a, b) for a in (-1, 0, 1) for b in (-1, 0, 1) if (a, b) != (0, 0)]
OFFSETS = [(a, b) for a in (-1, 0, 1) for b in (-1, 0, 1)]


def lane_dips(dips, rows, cols):
    lanes = rows * cols
    col = lax.broadcasted_iota(jnp.int32, (cols, lanes), 0)
    lane = lax.broadcasted_iota(jnp.int32, (cols, lanes), 1)
    spread = jnp.where(lane % cols == col, 1.0, 0.0).astype(jnp.float32)
    tiled = jnp.dot(dips.astype(jnp.float32), spread, preferred_element_type=jnp.float32)
    row = lax.broadcasted_iota(jnp.int32, (rows, lanes), 0)
    here = lax.broadcasted_iota(jnp.int32, (rows, lanes), 1) // cols == row
    return jnp.sum(jnp.where(here, tiled, 0.0), axis=0, keepdims=True)


def select_shift(rows, shift, reach):
    left = shift + float(reach)
    step = 8 if reach > 3 else 4
    while step:
        on = left >= float(step)
        left = jnp.where(on, left - float(step), left)
        count = len(rows) - step if step > 1 else CHUNK
        keep = min(count, len(rows))
        need = CHUNK + step - 1
        rows = [
            jnp.where(on, rows[k + step], rows[k]) if k + step < len(rows) else rows[k]
            for k in range(min(len(rows), need))
        ]
        step //= 2
    return rows[:CHUNK]


def steer_kernel(
    rows, cols, vintages, inlines, xlines,
    amp, dip_il, dip_xl, attr, base, semb_t,
    tile, times, d_il, d_xl,
    load_sem, halo_send, halo_recv, base_send, base_recv,
):
    v = lax.axis_index("vintage")
    i = lax.axis_index("inline")
    x = lax.axis_index("xline")
    loads = [
        pltpu.make_async_copy(amp.at[0], tile.at[pl.ds(1, rows), pl.ds(PAD, cols), :], load_sem.at[0]),
        pltpu.make_async_copy(dip_il.at[0], d_il, load_sem.at[1]),
        pltpu.make_async_copy(dip_xl.at[0], d_xl, load_sem.at[2]),
    ]
    for load in loads:
        load.start()

    edge = jnp.zeros((PAD, TIME_SAMPLES), jnp.float32)
    for row in range(rows + 2):
        tile[row, 0:PAD, :] = edge
        tile[row, PAD + cols : 2 * PAD + cols, :] = edge
    for row in (0, rows + 1):
        tile[row, PAD : PAD + cols, :] = jnp.zeros((cols, TIME_SAMPLES), jnp.float32)

    def inside(a, b):
        return (i + a >= 0) & (i + a < inlines) & (x + b >= 0) & (x + b < xlines)

    barrier = pltpu.get_barrier_semaphore()
    greeted = jnp.int32(0)
    for a, b in DIRECTIONS:
        there = inside(a, b)
        greeted = greeted + jnp.where(there, 1, 0)

        @pl.when(there)
        def _():
            pl.semaphore_signal(
                barrier, inc=1, device_id={"inline": i + a, "xline": x + b}, device_id_type=MESH
            )

    direct = [other for other in range(1, vintages) if other == 1 or other % 2 == 0]
    passes_on = (v % 2 == 0) & (v > 0) & (v + 1 < vintages)

    @pl.when(v != 0)
    def _():
        parent = jnp.where((v % 2 == 1) & (v > 1), v - 1, 0)
        pl.semaphore_signal(barrier, inc=1, device_id={"vintage": parent}, device_id_type=MESH)

    greeted = greeted + jnp.where(v == 0, len(direct), 0) + jnp.where(passes_on, 1, 0)
    pl.semaphore_wait(barrier, greeted)

    def halo(index):
        a, b = DIRECTIONS[index]
        row_from = {-1: pl.ds(0, 1), 0: pl.ds(0, rows), 1: pl.ds(rows - 1, 1)}[a]
        row_to = {-1: pl.ds(rows + 1, 1), 0: pl.ds(1, rows), 1: pl.ds(0, 1)}[a]
        col_from = {-1: pl.ds(0, PAD), 0: pl.ds(0, cols), 1: pl.ds(cols - PAD, PAD)}[b]
        col_to = {-1: pl.ds(PAD + cols, PAD), 0: pl.ds(PAD, cols), 1: pl.ds(0, PAD)}[b]
        return pltpu.make_async_remote_copy(
            src_ref=amp.at[0, row_from, col_from, :],
            dst_ref=tile.at[row_to, col_to, :],
            send_sem=halo_send.at[index],
            recv_sem=halo_recv.at[index],
            device_id={"inline": i + a, "xline": x + b},
            device_id_type=MESH,
        )

    for index, (a, b) in enumerate(DIRECTIONS):

        @pl.when(inside(a, b))
        def _():
            halo(index).start()

    for load in loads:
        load.wait()
    dips = [lane_dips(d_il[...], rows, cols), lane_dips(d_xl[...], rows, cols)]
    lanes = rows * cols
    dips = [jnp.broadcast_to(dip, (NWIN, lanes)) for dip in dips]
    blank = jnp.zeros((PAD, lanes), jnp.float32)
    for slot in range(len(OFFSETS)):
        times[slot, 0:PAD, :] = blank
        times[slot, PAD + TIME_SAMPLES : 2 * PAD + TIME_SAMPLES, :] = blank

    for index, (a, b) in enumerate(DIRECTIONS):

        @pl.when(inside(-a, -b))
        def _():
            halo(index).wait_recv()

    for slot, (a, b) in enumerate(OFFSETS):
        block = tile[1 + a : 1 + a + rows, PAD + b : PAD + b + cols, :]
        times[slot, PAD : PAD + TIME_SAMPLES, :] = block.reshape(lanes, TIME_SAMPLES).T

    def stack_chunk(chunk):
        first = chunk * CHUNK
        total = [None] * CHUNK
        squares = [None] * CHUNK
        for slot, (a, b) in enumerate(OFFSETS):
            reach = (abs(a) + abs(b)) * MAX_DIP_STEP
            taps = [
                times[slot, pl.ds(first + REACH - reach + k, NWIN, stride=WIN), :]
                for k in range(CHUNK + 2 * reach)
            ]
            moved = taps
            if reach:
                moved = select_shift(taps, float(a) * dips[0] + float(b) * dips[1], reach)
            for k in range(CHUNK):
                square = moved[k] * moved[k]
                total[k] = moved[k] if total[k] is None else total[k] + moved[k]
                squares[k] = square if squares[k] is None else squares[k] + square
        return total, squares

    def window(values):
        twos = [values[k] + values[k + 1] for k in range(len(values) - 1)]
        fours = [twos[k] + twos[k + 2] for k in range(len(twos) - 2)]
        return [fours[k] + fours[k + 4] + values[k + 8] for k in range(CHUNK)]

    def share(chunk, other):
        return pltpu.make_async_remote_copy(
            src_ref=attr.at[pl.ds(chunk * CHUNK, CHUNK)],
            dst_ref=base.at[pl.ds(chunk * CHUNK, CHUNK)],
            send_sem=base_send.at[chunk, direct.index(other)],
            recv_sem=base_recv.at[chunk],
            device_id={"vintage": other},
            device_id_type=MESH,
        )

    def pass_on(chunk):
        return pltpu.make_async_remote_copy(
            src_ref=base.at[pl.ds(chunk * CHUNK, CHUNK)],
            dst_ref=base.at[pl.ds(chunk * CHUNK, CHUNK)],
            send_sem=base_send.at[chunk, 0],
            recv_sem=base_recv.at[chunk],
            device_id={"vintage": v + 1},
            device_id_type=MESH,
        )

    def attribute_chunk(chunk, carried):
        total, squares = stack_chunk(chunk + 1)
        first = chunk * CHUNK
        sums = list(carried[0]) + total
        numer = window([s * s for s in sums])
        denom = window(list(carried[1]) + squares)
        for k in range(CHUNK):
            semb = numer[k] / (9.0 * denom[k] + EPS)
            semb_t[pl.ds(first + k, NWIN, stride=WIN), :] = semb
            attr[first + k] = semb * sums[RT + k] * (1.0 / 9.0)

        @pl.when(v == 0)
        def _():
            for other in direct:
                share(chunk, other).start()

        return total, squares

    lax.fori_loop(0, CHUNKS, attribute_chunk, stack_chunk(0))

    @pl.when(v == 0)
    def _():
        base[...] = attr[...]

    @pl.when(v != 0)
    def _():
        for chunk in range(CHUNKS):
            pass_on(chunk).wait_recv()

            @pl.when(passes_on)
            def _():
                pass_on(chunk).start()

    for index, (a, b) in enumerate(DIRECTIONS):

        @pl.when(inside(a, b))
        def _():
            halo(index).wait_send()

    @pl.when(v == 0)
    def _():
        for chunk in range(CHUNKS):
            for other in direct:
                share(chunk, other).wait_send()

    @pl.when(passes_on)
    def _():
        for chunk in range(CHUNKS):
            pass_on(chunk).wait_send()


def correlate_kernel(
    attr, base, semb_t, semb_out, corr_out, wide, semb_n, corr_t, corr_n, store_sem
):
    lanes = attr.shape[2]
    semb_n[...] = semb_t[...].T
    semb_store = pltpu.make_async_copy(semb_n, semb_out, store_sem.at[0])
    semb_store.start()

    win = lax.broadcasted_iota(jnp.int32, (NWIN, lanes), 0)
    for k in range(WIN):
        wide[HALF + k] = base[k]
    for k in range(HALF):
        wide[k] = jnp.where(win == 0, 0.0, pltpu.roll(base[k + WIN - HALF], 1, 0))
        wide[HALF + WIN + k] = jnp.where(win == NWIN - 1, 0.0, pltpu.roll(base[k], NWIN - 1, 0))

    def energy(ref):
        parts = [ref[k] * ref[k] for k in range(WIN)]
        while len(parts) > 1:
            parts = [parts[k] + parts[k + 1] for k in range(0, len(parts), 2)]
        return jnp.sum(parts[0], axis=0, keepdims=True)

    factor = NWIN / jnp.sqrt(energy(attr) * energy(base) + EPS)
    factor = jnp.broadcast_to(factor, (NWIN, lanes))

    def add_chunk(chunk, acc):
        first = chunk * CHUNK
        mine = [attr[first + k] for k in range(CHUNK)]
        acc = list(acc)
        for j in range(CHUNK + LAGS - 1):
            other = wide[first + j]
            for k in range(CHUNK):
                if 0 <= j - k < LAGS:
                    acc[j - k] = acc[j - k] + mine[k] * other
        return tuple(acc)

    zero = jnp.zeros((NWIN, lanes), jnp.float32)
    acc = lax.fori_loop(0, CHUNKS, add_chunk, (zero,) * LAGS)
    for lag in range(LAGS):
        corr_t[lag * NWIN : (lag + 1) * NWIN, :] = acc[lag] * factor
    corr_n[:, 0:TIME_SAMPLES] = corr_t[0:TIME_SAMPLES, :].T
    corr_n[:, TIME_SAMPLES : LAGS * NWIN] = corr_t[TIME_SAMPLES : LAGS * NWIN, :].T
    corr_store = pltpu.make_async_copy(corr_n, corr_out, store_sem.at[1])
    corr_store.start()
    semb_store.wait()
    corr_store.wait()


def per_device(vintages, inlines, xlines, amplitude, inline_slope, crossline_slope):
    _, rows, cols, _ = amplitude.shape
    lanes = rows * cols
    f32 = jnp.float32
    in_hbm = pl.BlockSpec(memory_space=pltpu.HBM)
    in_vmem = pl.BlockSpec(memory_space=pltpu.VMEM)
    operands = [
        pltpu.with_memory_space_constraint(array, pltpu.HBM)
        for array in (amplitude, inline_slope, crossline_slope)
    ]
    held = pl.pallas_call(
        functools.partial(steer_kernel, rows, cols, vintages, inlines, xlines),
        out_shape=(
            pltpu.VMEM((WIN, NWIN, lanes), f32),
            pltpu.VMEM((WIN, NWIN, lanes), f32),
            pltpu.VMEM((TIME_SAMPLES, lanes), f32),
        ),
        in_specs=[in_hbm] * 3,
        out_specs=(in_vmem,) * 3,
        scratch_shapes=[
            pltpu.VMEM((rows + 2, cols + 2 * PAD, TIME_SAMPLES), f32),
            pltpu.VMEM((len(OFFSETS), TIME_SAMPLES + 2 * PAD, lanes), f32),
            pltpu.VMEM((rows, cols), jnp.int32),
            pltpu.VMEM((rows, cols), jnp.int32),
            pltpu.SemaphoreType.DMA((3,)),
            pltpu.SemaphoreType.DMA((len(DIRECTIONS),)),
            pltpu.SemaphoreType.DMA((len(DIRECTIONS),)),
            pltpu.SemaphoreType.DMA((CHUNKS, max(vintages // 2 + 1, 1))),
            pltpu.SemaphoreType.DMA((CHUNKS,)),
        ],
        compiler_params=pltpu.CompilerParams(
            collective_id=0, has_side_effects=True, vmem_limit_bytes=16 * 2**20
        ),
        name="steer",
    )(*operands)
    semb, correl = pl.pallas_call(
        correlate_kernel,
        out_shape=(
            pltpu.HBM((lanes, TIME_SAMPLES), f32),
            pltpu.HBM((lanes, LAGS * NWIN), f32),
        ),
        in_specs=[in_vmem] * 3,
        out_specs=(in_hbm, in_hbm),
        scratch_shapes=[
            pltpu.VMEM((WIN + 2 * HALF, NWIN, lanes), f32),
            pltpu.VMEM((lanes, TIME_SAMPLES), f32),
            pltpu.VMEM((LAGS * NWIN, lanes), f32),
            pltpu.VMEM((lanes, LAGS * NWIN), f32),
            pltpu.SemaphoreType.DMA((2,)),
        ],
        compiler_params=pltpu.CompilerParams(vmem_limit_bytes=16 * 2**20),
        name="correlate",
    )(*[pltpu.with_memory_space_constraint(array, pltpu.VMEM) for array in held])
    return (
        semb.reshape(1, rows, cols, TIME_SAMPLES),
        correl.reshape(1, rows, cols, LAGS * NWIN),
    )


def solution(mesh):
    sizes = [mesh.shape[axis] for axis in ("vintage", "inline", "xline")]
    return jax.shard_map(
        functools.partial(per_device, *sizes),
        mesh=mesh,
        in_specs=(
            P("vintage", "inline", "xline", None),
            P("vintage", "inline", "xline"),
            P("vintage", "inline", "xline"),
        ),
        out_specs=(P("vintage", "inline", "xline", None), P("vintage", "inline", "xline", None)),
        check_vma=False,
    )
```

```python
import functools

import jax
import jax.numpy as jnp
from jax import lax
from jax.experimental import pallas as pl
from jax.experimental.pallas import tpu as pltpu
from jax.sharding import PartitionSpec as P

TIME_SAMPLES = 256
MAX_DIP_STEP = 2
RT = 4
LAGS = 33
NWIN = 8
EPS = 1e-06

WIN = TIME_SAMPLES // NWIN
HALF = LAGS // 2
REACH = 2 * MAX_DIP_STEP
PAD = 8
CHUNK = 8
CHUNKS = WIN // CHUNK
MESH = pl.DeviceIdType.MESH
DIRECTIONS = [(-1, -1), (-1, 1), (1, -1), (1, 1), (0, -1), (0, 1), (-1, 0), (1, 0)]
OFFSETS = [(a, b) for a in (-1, 0, 1) for b in (-1, 0, 1)]


def lane_dips(dips, rows, cols):
    lanes = rows * cols
    col = lax.broadcasted_iota(jnp.int32, (cols, lanes), 0)
    lane = lax.broadcasted_iota(jnp.int32, (cols, lanes), 1)
    spread = jnp.where(lane % cols == col, 1.0, 0.0).astype(jnp.float32)
    tiled = jnp.dot(dips.astype(jnp.float32), spread, preferred_element_type=jnp.float32)
    row = lax.broadcasted_iota(jnp.int32, (rows, lanes), 0)
    here = lax.broadcasted_iota(jnp.int32, (rows, lanes), 1) // cols == row
    return jnp.sum(jnp.where(here, tiled, 0.0), axis=0, keepdims=True)


def select_shift(rows, shift, reach):
    left = shift + float(reach)
    step = 8 if reach > 3 else 4
    while step:
        on = left >= float(step)
        left = jnp.where(on, left - float(step), left)
        count = len(rows) - step if step > 1 else CHUNK
        keep = min(count, len(rows))
        need = CHUNK + step - 1
        rows = [
            jnp.where(on, rows[k + step], rows[k]) if k + step < len(rows) else rows[k]
            for k in range(min(len(rows), need))
        ]
        step //= 2
    return rows[:CHUNK]


def steer_kernel(
    rows, cols, vintages, inlines, xlines,
    amp, dip_il, dip_xl, attr, base, semb_n,
    tile, times, semb_t, d_il, d_xl,
    load_sem, halo_send, halo_recv, base_send, base_recv,
):
    v = lax.axis_index("vintage")
    i = lax.axis_index("inline")
    x = lax.axis_index("xline")
    loads = [
        pltpu.make_async_copy(amp.at[0], tile.at[pl.ds(1, rows), pl.ds(PAD, cols), :], load_sem.at[0]),
        pltpu.make_async_copy(dip_il.at[0], d_il, load_sem.at[1]),
        pltpu.make_async_copy(dip_xl.at[0], d_xl, load_sem.at[2]),
    ]
    for load in loads:
        load.start()

    edge = jnp.zeros((PAD, TIME_SAMPLES), jnp.float32)
    for row in range(rows + 2):
        tile[row, 0:PAD, :] = edge
        tile[row, PAD + cols : 2 * PAD + cols, :] = edge
    for row in (0, rows + 1):
        tile[row, PAD : PAD + cols, :] = jnp.zeros((cols, TIME_SAMPLES), jnp.float32)

    def inside(a, b):
        return (i + a >= 0) & (i + a < inlines) & (x + b >= 0) & (x + b < xlines)

    barrier = pltpu.get_barrier_semaphore()
    greeted = jnp.int32(0)
    for a, b in DIRECTIONS:
        there = inside(a, b)
        greeted = greeted + jnp.where(there, 1, 0)

        @pl.when(there)
        def _():
            pl.semaphore_signal(
                barrier, inc=1, device_id={"inline": i + a, "xline": x + b}, device_id_type=MESH
            )

    direct = [other for other in range(1, vintages) if other == 1 or other % 2 == 0]
    passes_on = (v % 2 == 0) & (v > 0) & (v + 1 < vintages)

    @pl.when(v != 0)
    def _():
        parent = jnp.where((v % 2 == 1) & (v > 1), v - 1, 0)
        pl.semaphore_signal(barrier, inc=1, device_id={"vintage": parent}, device_id_type=MESH)

    greeted = greeted + jnp.where(v == 0, len(direct), 0) + jnp.where(passes_on, 1, 0)
    pl.semaphore_wait(barrier, greeted)

    def halo(index):
        a, b = DIRECTIONS[index]
        row_from = {-1: pl.ds(0, 1), 0: pl.ds(0, rows), 1: pl.ds(rows - 1, 1)}[a]
        row_to = {-1: pl.ds(rows + 1, 1), 0: pl.ds(1, rows), 1: pl.ds(0, 1)}[a]
        col_from = {-1: pl.ds(0, 1), 0: pl.ds(0, cols), 1: pl.ds(cols - 1, 1)}[b]
        col_to = {-1: pl.ds(PAD + cols, 1), 0: pl.ds(PAD, cols), 1: pl.ds(PAD - 1, 1)}[b]
        return pltpu.make_async_remote_copy(
            src_ref=amp.at[0, row_from, col_from, :],
            dst_ref=tile.at[row_to, col_to, :],
            send_sem=halo_send.at[index],
            recv_sem=halo_recv.at[index],
            device_id={"inline": i + a, "xline": x + b},
            device_id_type=MESH,
        )

    for index, (a, b) in enumerate(DIRECTIONS):

        @pl.when(inside(a, b))
        def _():
            halo(index).start()

    for load in loads:
        load.wait()
    dips = [lane_dips(d_il[...], rows, cols), lane_dips(d_xl[...], rows, cols)]
    lanes = rows * cols
    dips = [jnp.broadcast_to(dip, (NWIN, lanes)) for dip in dips]
    blank = jnp.zeros((PAD, lanes), jnp.float32)
    for slot in range(len(OFFSETS)):
        times[slot, 0:PAD, :] = blank
        times[slot, PAD + TIME_SAMPLES : 2 * PAD + TIME_SAMPLES, :] = blank

    def turn(a, b):
        block = tile[1 + a : 1 + a + rows, PAD + b : PAD + b + cols, :]
        slot = OFFSETS.index((a, b))
        times[slot, PAD : PAD + TIME_SAMPLES, :] = block.reshape(lanes, TIME_SAMPLES).T

    turn(0, 0)
    for index in range(len(DIRECTIONS) - 1, -1, -1):
        a, b = DIRECTIONS[index]

        @pl.when(inside(-a, -b))
        def _():
            halo(index).wait_recv()

        turn(-a, -b)

    def stack_chunk(chunk):
        first = chunk * CHUNK
        total = [None] * CHUNK
        squares = [None] * CHUNK
        for slot, (a, b) in enumerate(OFFSETS):
            reach = (abs(a) + abs(b)) * MAX_DIP_STEP
            taps = [
                times[slot, pl.ds(first + REACH - reach + k, NWIN, stride=WIN), :]
                for k in range(CHUNK + 2 * reach)
            ]
            moved = taps
            if reach:
                moved = select_shift(taps, float(a) * dips[0] + float(b) * dips[1], reach)
            for k in range(CHUNK):
                square = moved[k] * moved[k]
                total[k] = moved[k] if total[k] is None else total[k] + moved[k]
                squares[k] = square if squares[k] is None else squares[k] + square
        return total, squares

    def window(values):
        twos = [values[k] + values[k + 1] for k in range(len(values) - 1)]
        fours = [twos[k] + twos[k + 2] for k in range(len(twos) - 2)]
        return [fours[k] + fours[k + 4] + values[k + 8] for k in range(CHUNK)]

    def share(chunk, other):
        return pltpu.make_async_remote_copy(
            src_ref=attr.at[pl.ds(chunk * CHUNK, CHUNK)],
            dst_ref=base.at[pl.ds(chunk * CHUNK, CHUNK)],
            send_sem=base_send.at[chunk, direct.index(other)],
            recv_sem=base_recv.at[chunk],
            device_id={"vintage": other},
            device_id_type=MESH,
        )

    def pass_on(chunk):
        return pltpu.make_async_remote_copy(
            src_ref=base.at[pl.ds(chunk * CHUNK, CHUNK)],
            dst_ref=base.at[pl.ds(chunk * CHUNK, CHUNK)],
            send_sem=base_send.at[chunk, 0],
            recv_sem=base_recv.at[chunk],
            device_id={"vintage": v + 1},
            device_id_type=MESH,
        )

    def attribute_chunk(chunk, carried):
        total, squares = stack_chunk(chunk + 1)
        first = chunk * CHUNK
        sums = list(carried[0]) + total
        numer = window([s * s for s in sums])
        denom = window(list(carried[1]) + squares)
        for k in range(CHUNK):
            semb = numer[k] / (9.0 * denom[k] + EPS)
            semb_t[pl.ds(first + k, NWIN, stride=WIN), :] = semb
            attr[first + k] = semb * sums[RT + k] * (1.0 / 9.0)

        @pl.when(v == 0)
        def _():
            for other in direct:
                share(chunk, other).start()

        return total, squares

    lax.fori_loop(0, CHUNKS, attribute_chunk, stack_chunk(0))

    semb_n[...] = semb_t[...].T

    @pl.when(v == 0)
    def _():
        base[...] = attr[...]

    @pl.when(v != 0)
    def _():
        for chunk in range(CHUNKS):
            pass_on(chunk).wait_recv()

            @pl.when(passes_on)
            def _():
                pass_on(chunk).start()

    for index, (a, b) in enumerate(DIRECTIONS):

        @pl.when(inside(a, b))
        def _():
            halo(index).wait_send()

    @pl.when(v == 0)
    def _():
        for chunk in range(CHUNKS):
            for other in direct:
                share(chunk, other).wait_send()

    @pl.when(passes_on)
    def _():
        for chunk in range(CHUNKS):
            pass_on(chunk).wait_send()


def correlate_kernel(
    attr, base, semb_n, semb_out, corr_out, wide, corr_t, corr_n, store_sem
):
    lanes = attr.shape[2]
    semb_store = pltpu.make_async_copy(semb_n, semb_out, store_sem.at[0])
    semb_store.start()

    win = lax.broadcasted_iota(jnp.int32, (NWIN, lanes), 0)
    for k in range(WIN):
        wide[HALF + k] = base[k]
    for k in range(HALF):
        wide[k] = jnp.where(win == 0, 0.0, pltpu.roll(base[k + WIN - HALF], 1, 0))
        wide[HALF + WIN + k] = jnp.where(win == NWIN - 1, 0.0, pltpu.roll(base[k], NWIN - 1, 0))

    def energy(ref):
        parts = [ref[k] * ref[k] for k in range(WIN)]
        while len(parts) > 1:
            parts = [parts[k] + parts[k + 1] for k in range(0, len(parts), 2)]
        return jnp.sum(parts[0], axis=0, keepdims=True)

    factor = NWIN / jnp.sqrt(energy(attr) * energy(base) + EPS)
    factor = jnp.broadcast_to(factor, (NWIN, lanes))

    def add_chunk(chunk, acc):
        first = chunk * CHUNK
        mine = [attr[first + k] for k in range(CHUNK)]
        acc = list(acc)
        for j in range(CHUNK + LAGS - 1):
            other = wide[first + j]
            for k in range(CHUNK):
                if 0 <= j - k < LAGS:
                    acc[j - k] = acc[j - k] + mine[k] * other
        return tuple(acc)

    zero = jnp.zeros((NWIN, lanes), jnp.float32)
    acc = lax.fori_loop(0, CHUNKS, add_chunk, (zero,) * LAGS)
    for lag in range(LAGS):
        corr_t[lag * NWIN : (lag + 1) * NWIN, :] = acc[lag] * factor
    corr_n[:, 0:TIME_SAMPLES] = corr_t[0:TIME_SAMPLES, :].T
    corr_n[:, TIME_SAMPLES : LAGS * NWIN] = corr_t[TIME_SAMPLES : LAGS * NWIN, :].T
    corr_store = pltpu.make_async_copy(corr_n, corr_out, store_sem.at[1])
    corr_store.start()
    semb_store.wait()
    corr_store.wait()


def per_device(vintages, inlines, xlines, amplitude, inline_slope, crossline_slope):
    _, rows, cols, _ = amplitude.shape
    lanes = rows * cols
    f32 = jnp.float32
    in_hbm = pl.BlockSpec(memory_space=pltpu.HBM)
    in_vmem = pl.BlockSpec(memory_space=pltpu.VMEM)
    operands = [
        pltpu.with_memory_space_constraint(array, pltpu.HBM)
        for array in (amplitude, inline_slope, crossline_slope)
    ]
    held = pl.pallas_call(
        functools.partial(steer_kernel, rows, cols, vintages, inlines, xlines),
        out_shape=(
            pltpu.VMEM((WIN, NWIN, lanes), f32),
            pltpu.VMEM((WIN, NWIN, lanes), f32),
            pltpu.VMEM((lanes, TIME_SAMPLES), f32),
        ),
        in_specs=[in_hbm] * 3,
        out_specs=(in_vmem,) * 3,
        scratch_shapes=[
            pltpu.VMEM((rows + 2, cols + 2 * PAD, TIME_SAMPLES), f32),
            pltpu.VMEM((len(OFFSETS), TIME_SAMPLES + 2 * PAD, lanes), f32),
            pltpu.VMEM((TIME_SAMPLES, lanes), f32),
            pltpu.VMEM((rows, cols), jnp.int32),
            pltpu.VMEM((rows, cols), jnp.int32),
            pltpu.SemaphoreType.DMA((3,)),
            pltpu.SemaphoreType.DMA((len(DIRECTIONS),)),
            pltpu.SemaphoreType.DMA((len(DIRECTIONS),)),
            pltpu.SemaphoreType.DMA((CHUNKS, max(vintages // 2 + 1, 1))),
            pltpu.SemaphoreType.DMA((CHUNKS,)),
        ],
        compiler_params=pltpu.CompilerParams(
            collective_id=0, has_side_effects=True, vmem_limit_bytes=16 * 2**20
        ),
        name="steer",
    )(*operands)
    semb, correl = pl.pallas_call(
        correlate_kernel,
        out_shape=(
            pltpu.HBM((lanes, TIME_SAMPLES), f32),
            pltpu.HBM((lanes, LAGS * NWIN), f32),
        ),
        in_specs=[in_vmem] * 3,
        out_specs=(in_hbm, in_hbm),
        scratch_shapes=[
            pltpu.VMEM((WIN + 2 * HALF, NWIN, lanes), f32),
            pltpu.VMEM((LAGS * NWIN, lanes), f32),
            pltpu.VMEM((lanes, LAGS * NWIN), f32),
            pltpu.SemaphoreType.DMA((2,)),
        ],
        compiler_params=pltpu.CompilerParams(vmem_limit_bytes=16 * 2**20),
        name="correlate",
    )(*[pltpu.with_memory_space_constraint(array, pltpu.VMEM) for array in held])
    return (
        semb.reshape(1, rows, cols, TIME_SAMPLES),
        correl.reshape(1, rows, cols, LAGS * NWIN),
    )


def solution(mesh):
    sizes = [mesh.shape[axis] for axis in ("vintage", "inline", "xline")]
    return jax.shard_map(
        functools.partial(per_device, *sizes),
        mesh=mesh,
        in_specs=(
            P("vintage", "inline", "xline", None),
            P("vintage", "inline", "xline"),
            P("vintage", "inline", "xline"),
        ),
        out_specs=(P("vintage", "inline", "xline", None), P("vintage", "inline", "xline", None)),
        check_vma=False,
    )
```

```python
import functools

import jax
import jax.numpy as jnp
from jax import lax
from jax.experimental import pallas as pl
from jax.experimental.pallas import tpu as pltpu
from jax.sharding import PartitionSpec as P

TIME_SAMPLES = 256
MAX_DIP_STEP = 2
RT = 4
LAGS = 33
NWIN = 8
EPS = 1e-06

WIN = TIME_SAMPLES // NWIN
HALF = LAGS // 2
REACH = 2 * MAX_DIP_STEP
PAD = 8
CHUNK = 8
CHUNKS = WIN // CHUNK
MESH = pl.DeviceIdType.MESH
DIRECTIONS = [(-1, -1), (-1, 1), (1, -1), (1, 1), (0, -1), (0, 1), (-1, 0), (1, 0)]
OFFSETS = [(a, b) for a in (-1, 0, 1) for b in (-1, 0, 1)]


def lane_dips(dips, rows, cols):
    lanes = rows * cols
    col = lax.broadcasted_iota(jnp.int32, (cols, lanes), 0)
    lane = lax.broadcasted_iota(jnp.int32, (cols, lanes), 1)
    spread = jnp.where(lane % cols == col, 1.0, 0.0).astype(jnp.float32)
    tiled = jnp.dot(dips.astype(jnp.float32), spread, preferred_element_type=jnp.float32)
    row = lax.broadcasted_iota(jnp.int32, (rows, lanes), 0)
    here = lax.broadcasted_iota(jnp.int32, (rows, lanes), 1) // cols == row
    return jnp.sum(jnp.where(here, tiled, 0.0), axis=0, keepdims=True)


def select_shift(rows, shift, reach):
    left = shift + float(reach)
    step = 8 if reach > 3 else 4
    while step:
        on = left >= float(step)
        left = jnp.where(on, left - float(step), left)
        count = len(rows) - step if step > 1 else CHUNK
        keep = min(count, len(rows))
        need = CHUNK + step - 1
        rows = [
            jnp.where(on, rows[k + step], rows[k]) if k + step < len(rows) else rows[k]
            for k in range(min(len(rows), need))
        ]
        step //= 2
    return rows[:CHUNK]


def steer_kernel(
    rows, cols, vintages, inlines, xlines,
    amp, dip_il, dip_xl, attr, base, semb_n,
    tile, times, rows_of, semb_t, d_il, d_xl,
    load_sem, halo_send, halo_recv, base_send, base_recv,
):
    v = lax.axis_index("vintage")
    i = lax.axis_index("inline")
    x = lax.axis_index("xline")
    loads = [
        pltpu.make_async_copy(amp.at[0], tile.at[pl.ds(1, rows), pl.ds(PAD, cols), :], load_sem.at[0]),
        pltpu.make_async_copy(dip_il.at[0], d_il, load_sem.at[1]),
        pltpu.make_async_copy(dip_xl.at[0], d_xl, load_sem.at[2]),
    ]
    for load in loads:
        load.start()

    edge = jnp.zeros((PAD, TIME_SAMPLES), jnp.float32)
    for row in range(rows + 2):
        tile[row, 0:PAD, :] = edge
        tile[row, PAD + cols : 2 * PAD + cols, :] = edge
    for row in (0, rows + 1):
        tile[row, PAD : PAD + cols, :] = jnp.zeros((cols, TIME_SAMPLES), jnp.float32)

    def inside(a, b):
        return (i + a >= 0) & (i + a < inlines) & (x + b >= 0) & (x + b < xlines)

    barrier = pltpu.get_barrier_semaphore()
    greeted = jnp.int32(0)
    for a, b in DIRECTIONS:
        there = inside(a, b)
        greeted = greeted + jnp.where(there, 1, 0)

        @pl.when(there)
        def _():
            pl.semaphore_signal(
                barrier, inc=1, device_id={"inline": i + a, "xline": x + b}, device_id_type=MESH
            )

    direct = [other for other in range(1, vintages) if other == 1 or other % 2 == 0]
    passes_on = (v % 2 == 0) & (v > 0) & (v + 1 < vintages)

    @pl.when(v != 0)
    def _():
        parent = jnp.where((v % 2 == 1) & (v > 1), v - 1, 0)
        pl.semaphore_signal(barrier, inc=1, device_id={"vintage": parent}, device_id_type=MESH)

    greeted = greeted + jnp.where(v == 0, len(direct), 0) + jnp.where(passes_on, 1, 0)
    pl.semaphore_wait(barrier, greeted)

    def halo(index):
        a, b = DIRECTIONS[index]
        row_from = {-1: pl.ds(0, 1), 0: pl.ds(0, rows), 1: pl.ds(rows - 1, 1)}[a]
        row_to = {-1: pl.ds(rows + 1, 1), 0: pl.ds(1, rows), 1: pl.ds(0, 1)}[a]
        col_from = {-1: pl.ds(0, PAD), 0: pl.ds(0, cols), 1: pl.ds(cols - PAD, PAD)}[b]
        col_to = {-1: pl.ds(PAD + cols, PAD), 0: pl.ds(PAD, cols), 1: pl.ds(0, PAD)}[b]
        return pltpu.make_async_remote_copy(
            src_ref=amp.at[0, row_from, col_from, :],
            dst_ref=tile.at[row_to, col_to, :],
            send_sem=halo_send.at[index],
            recv_sem=halo_recv.at[index],
            device_id={"inline": i + a, "xline": x + b},
            device_id_type=MESH,
        )

    for index, (a, b) in enumerate(DIRECTIONS):

        @pl.when(inside(a, b))
        def _():
            halo(index).start()

    for load in loads:
        load.wait()
    dips = [lane_dips(d_il[...], rows, cols), lane_dips(d_xl[...], rows, cols)]
    lanes = rows * cols
    dips = [jnp.broadcast_to(dip, (NWIN, lanes)) for dip in dips]
    win = lax.broadcasted_iota(jnp.int32, (NWIN, lanes), 0)

    def turn(a, b):
        block = tile[1 + a : 1 + a + rows, PAD + b : PAD + b + cols, :]
        slot = OFFSETS.index((a, b))
        times[slot] = block.reshape(lanes, TIME_SAMPLES).T
        for r in range(WIN):
            taken = times[slot, pl.ds(r, NWIN, stride=WIN), :]
            rows_of[slot, PAD + r] = taken
            if r < PAD:
                later = jnp.where(win == NWIN - 1, 0.0, pltpu.roll(taken, NWIN - 1, 0))
                rows_of[slot, PAD + WIN + r] = later
            if r >= WIN - PAD:
                rows_of[slot, PAD + r - WIN] = jnp.where(win == 0, 0.0, pltpu.roll(taken, 1, 0))

    turn(0, 0)
    for index in range(len(DIRECTIONS) - 1, -1, -1):
        a, b = DIRECTIONS[index]

        @pl.when(inside(-a, -b))
        def _():
            halo(index).wait_recv()

        turn(-a, -b)

    def stack_chunk(chunk):
        first = chunk * CHUNK
        total = [None] * CHUNK
        squares = [None] * CHUNK
        for slot, (a, b) in enumerate(OFFSETS):
            reach = (abs(a) + abs(b)) * MAX_DIP_STEP
            taps = [
                rows_of[slot, first + REACH - reach + k]
                for k in range(CHUNK + 2 * reach)
            ]
            moved = taps
            if reach:
                moved = select_shift(taps, float(a) * dips[0] + float(b) * dips[1], reach)
            for k in range(CHUNK):
                square = moved[k] * moved[k]
                total[k] = moved[k] if total[k] is None else total[k] + moved[k]
                squares[k] = square if squares[k] is None else squares[k] + square
        return total, squares

    def window(values):
        twos = [values[k] + values[k + 1] for k in range(len(values) - 1)]
        fours = [twos[k] + twos[k + 2] for k in range(len(twos) - 2)]
        return [fours[k] + fours[k + 4] + values[k + 8] for k in range(CHUNK)]

    def share(chunk, other):
        return pltpu.make_async_remote_copy(
            src_ref=attr.at[pl.ds(chunk * CHUNK, CHUNK)],
            dst_ref=base.at[pl.ds(chunk * CHUNK, CHUNK)],
            send_sem=base_send.at[chunk, direct.index(other)],
            recv_sem=base_recv.at[chunk],
            device_id={"vintage": other},
            device_id_type=MESH,
        )

    def pass_on(chunk):
        return pltpu.make_async_remote_copy(
            src_ref=base.at[pl.ds(chunk * CHUNK, CHUNK)],
            dst_ref=base.at[pl.ds(chunk * CHUNK, CHUNK)],
            send_sem=base_send.at[chunk, 0],
            recv_sem=base_recv.at[chunk],
            device_id={"vintage": v + 1},
            device_id_type=MESH,
        )

    def attribute_chunk(chunk, carried):
        total, squares = stack_chunk(chunk + 1)
        first = chunk * CHUNK
        sums = list(carried[0]) + total
        numer = window([s * s for s in sums])
        denom = window(list(carried[1]) + squares)
        for k in range(CHUNK):
            semb = numer[k] / (9.0 * denom[k] + EPS)
            semb_t[pl.ds(first + k, NWIN, stride=WIN), :] = semb
            attr[first + k] = semb * sums[RT + k] * (1.0 / 9.0)

        @pl.when(v == 0)
        def _():
            for other in direct:
                share(chunk, other).start()

        return total, squares

    lax.fori_loop(0, CHUNKS, attribute_chunk, stack_chunk(0))

    semb_n[...] = semb_t[...].T

    @pl.when(v == 0)
    def _():
        base[...] = attr[...]

    @pl.when(v != 0)
    def _():
        for chunk in range(CHUNKS):
            pass_on(chunk).wait_recv()

            @pl.when(passes_on)
            def _():
                pass_on(chunk).start()

    for index, (a, b) in enumerate(DIRECTIONS):

        @pl.when(inside(a, b))
        def _():
            halo(index).wait_send()

    @pl.when(v == 0)
    def _():
        for chunk in range(CHUNKS):
            for other in direct:
                share(chunk, other).wait_send()

    @pl.when(passes_on)
    def _():
        for chunk in range(CHUNKS):
            pass_on(chunk).wait_send()


def correlate_kernel(
    attr, base, semb_n, semb_out, corr_out, wide, corr_t, corr_n, store_sem
):
    lanes = attr.shape[2]
    semb_store = pltpu.make_async_copy(semb_n, semb_out, store_sem.at[0])
    semb_store.start()

    win = lax.broadcasted_iota(jnp.int32, (NWIN, lanes), 0)
    for k in range(WIN):
        wide[HALF + k] = base[k]
    for k in range(HALF):
        wide[k] = jnp.where(win == 0, 0.0, pltpu.roll(base[k + WIN - HALF], 1, 0))
        wide[HALF + WIN + k] = jnp.where(win == NWIN - 1, 0.0, pltpu.roll(base[k], NWIN - 1, 0))

    def energy(ref):
        parts = [ref[k] * ref[k] for k in range(WIN)]
        while len(parts) > 1:
            parts = [parts[k] + parts[k + 1] for k in range(0, len(parts), 2)]
        return jnp.sum(parts[0], axis=0, keepdims=True)

    factor = NWIN / jnp.sqrt(energy(attr) * energy(base) + EPS)
    factor = jnp.broadcast_to(factor, (NWIN, lanes))

    def add_chunk(chunk, acc):
        first = chunk * CHUNK
        mine = [attr[first + k] for k in range(CHUNK)]
        acc = list(acc)
        for j in range(CHUNK + LAGS - 1):
            other = wide[first + j]
            for k in range(CHUNK):
                if 0 <= j - k < LAGS:
                    acc[j - k] = acc[j - k] + mine[k] * other
        return tuple(acc)

    zero = jnp.zeros((NWIN, lanes), jnp.float32)
    acc = lax.fori_loop(0, CHUNKS, add_chunk, (zero,) * LAGS)
    for lag in range(LAGS):
        corr_t[lag * NWIN : (lag + 1) * NWIN, :] = acc[lag] * factor
    corr_n[:, 0:TIME_SAMPLES] = corr_t[0:TIME_SAMPLES, :].T
    corr_n[:, TIME_SAMPLES : LAGS * NWIN] = corr_t[TIME_SAMPLES : LAGS * NWIN, :].T
    corr_store = pltpu.make_async_copy(corr_n, corr_out, store_sem.at[1])
    corr_store.start()
    semb_store.wait()
    corr_store.wait()


def per_device(vintages, inlines, xlines, amplitude, inline_slope, crossline_slope):
    _, rows, cols, _ = amplitude.shape
    lanes = rows * cols
    f32 = jnp.float32
    in_hbm = pl.BlockSpec(memory_space=pltpu.HBM)
    in_vmem = pl.BlockSpec(memory_space=pltpu.VMEM)
    operands = [
        pltpu.with_memory_space_constraint(array, pltpu.HBM)
        for array in (amplitude, inline_slope, crossline_slope)
    ]
    held = pl.pallas_call(
        functools.partial(steer_kernel, rows, cols, vintages, inlines, xlines),
        out_shape=(
            pltpu.VMEM((WIN, NWIN, lanes), f32),
            pltpu.VMEM((WIN, NWIN, lanes), f32),
            pltpu.VMEM((lanes, TIME_SAMPLES), f32),
        ),
        in_specs=[in_hbm] * 3,
        out_specs=(in_vmem,) * 3,
        scratch_shapes=[
            pltpu.VMEM((rows + 2, cols + 2 * PAD, TIME_SAMPLES), f32),
            pltpu.VMEM((len(OFFSETS), TIME_SAMPLES, lanes), f32),
            pltpu.VMEM((len(OFFSETS), WIN + 2 * PAD, NWIN, lanes), f32),
            pltpu.VMEM((TIME_SAMPLES, lanes), f32),
            pltpu.VMEM((rows, cols), jnp.int32),
            pltpu.VMEM((rows, cols), jnp.int32),
            pltpu.SemaphoreType.DMA((3,)),
            pltpu.SemaphoreType.DMA((len(DIRECTIONS),)),
            pltpu.SemaphoreType.DMA((len(DIRECTIONS),)),
            pltpu.SemaphoreType.DMA((CHUNKS, max(vintages // 2 + 1, 1))),
            pltpu.SemaphoreType.DMA((CHUNKS,)),
        ],
        compiler_params=pltpu.CompilerParams(
            collective_id=0, has_side_effects=True, vmem_limit_bytes=16 * 2**20
        ),
        name="steer",
    )(*operands)
    semb, correl = pl.pallas_call(
        correlate_kernel,
        out_shape=(
            pltpu.HBM((lanes, TIME_SAMPLES), f32),
            pltpu.HBM((lanes, LAGS * NWIN), f32),
        ),
        in_specs=[in_vmem] * 3,
        out_specs=(in_hbm, in_hbm),
        scratch_shapes=[
            pltpu.VMEM((WIN + 2 * HALF, NWIN, lanes), f32),
            pltpu.VMEM((LAGS * NWIN, lanes), f32),
            pltpu.VMEM((lanes, LAGS * NWIN), f32),
            pltpu.SemaphoreType.DMA((2,)),
        ],
        compiler_params=pltpu.CompilerParams(vmem_limit_bytes=16 * 2**20),
        name="correlate",
    )(*[pltpu.with_memory_space_constraint(array, pltpu.VMEM) for array in held])
    return (
        semb.reshape(1, rows, cols, TIME_SAMPLES),
        correl.reshape(1, rows, cols, LAGS * NWIN),
    )


def solution(mesh):
    sizes = [mesh.shape[axis] for axis in ("vintage", "inline", "xline")]
    return jax.shard_map(
        functools.partial(per_device, *sizes),
        mesh=mesh,
        in_specs=(
            P("vintage", "inline", "xline", None),
            P("vintage", "inline", "xline"),
            P("vintage", "inline", "xline"),
        ),
        out_specs=(P("vintage", "inline", "xline", None), P("vintage", "inline", "xline", None)),
        check_vma=False,
    )
```

```python
import functools

import jax
import jax.numpy as jnp
from jax import lax
from jax.experimental import pallas as pl
from jax.experimental.pallas import tpu as pltpu
from jax.sharding import PartitionSpec as P

TIME_SAMPLES = 256
MAX_DIP_STEP = 2
RT = 4
LAGS = 33
NWIN = 8
EPS = 1e-06

WIN = TIME_SAMPLES // NWIN
HALF = LAGS // 2
REACH = 2 * MAX_DIP_STEP
PAD = 8
CHUNK = 8
CHUNKS = WIN // CHUNK
MESH = pl.DeviceIdType.MESH
DIRECTIONS = [(-1, -1), (-1, 1), (1, -1), (1, 1), (0, -1), (0, 1), (-1, 0), (1, 0)]
OFFSETS = [(a, b) for a in (-1, 0, 1) for b in (-1, 0, 1)]


def lane_dips(dips, rows, cols):
    lanes = rows * cols
    col = lax.broadcasted_iota(jnp.int32, (cols, lanes), 0)
    lane = lax.broadcasted_iota(jnp.int32, (cols, lanes), 1)
    spread = jnp.where(lane % cols == col, 1.0, 0.0).astype(jnp.float32)
    tiled = jnp.dot(dips.astype(jnp.float32), spread, preferred_element_type=jnp.float32)
    row = lax.broadcasted_iota(jnp.int32, (rows, lanes), 0)
    here = lax.broadcasted_iota(jnp.int32, (rows, lanes), 1) // cols == row
    return jnp.sum(jnp.where(here, tiled, 0.0), axis=0, keepdims=True)


def select_shift(rows, shift, reach):
    left = shift + float(reach)
    step = 8 if reach > 3 else 4
    while step:
        on = left >= float(step)
        left = jnp.where(on, left - float(step), left)
        count = len(rows) - step if step > 1 else CHUNK
        keep = min(count, len(rows))
        need = CHUNK + step - 1
        rows = [
            jnp.where(on, rows[k + step], rows[k]) if k + step < len(rows) else rows[k]
            for k in range(min(len(rows), need))
        ]
        step //= 2
    return rows[:CHUNK]


def steer_kernel(
    rows, cols, vintages, inlines, xlines,
    amp, dip_il, dip_xl, semb_n, corr_n,
    tile, times, rows_of, semb_t, attr, base, corr_t, d_il, d_xl,
    load_sem, halo_send, halo_recv, base_send, base_recv,
):
    v = lax.axis_index("vintage")
    i = lax.axis_index("inline")
    x = lax.axis_index("xline")
    loads = [
        pltpu.make_async_copy(amp.at[0], tile.at[pl.ds(1, rows), pl.ds(PAD, cols), :], load_sem.at[0]),
        pltpu.make_async_copy(dip_il.at[0], d_il, load_sem.at[1]),
        pltpu.make_async_copy(dip_xl.at[0], d_xl, load_sem.at[2]),
    ]
    for load in loads:
        load.start()

    edge = jnp.zeros((PAD, TIME_SAMPLES), jnp.float32)
    for row in range(rows + 2):
        tile[row, 0:PAD, :] = edge
        tile[row, PAD + cols : 2 * PAD + cols, :] = edge
    for row in (0, rows + 1):
        tile[row, PAD : PAD + cols, :] = jnp.zeros((cols, TIME_SAMPLES), jnp.float32)

    def inside(a, b):
        return (i + a >= 0) & (i + a < inlines) & (x + b >= 0) & (x + b < xlines)

    barrier = pltpu.get_barrier_semaphore()
    greeted = jnp.int32(0)
    for a, b in DIRECTIONS:
        there = inside(a, b)
        greeted = greeted + jnp.where(there, 1, 0)

        @pl.when(there)
        def _():
            pl.semaphore_signal(
                barrier, inc=1, device_id={"inline": i + a, "xline": x + b}, device_id_type=MESH
            )

    direct = [other for other in range(1, vintages) if other == 1 or other % 2 == 0]
    passes_on = (v % 2 == 0) & (v > 0) & (v + 1 < vintages)

    @pl.when(v != 0)
    def _():
        parent = jnp.where((v % 2 == 1) & (v > 1), v - 1, 0)
        pl.semaphore_signal(barrier, inc=1, device_id={"vintage": parent}, device_id_type=MESH)

    greeted = greeted + jnp.where(v == 0, len(direct), 0) + jnp.where(passes_on, 1, 0)
    pl.semaphore_wait(barrier, greeted)

    def halo(index):
        a, b = DIRECTIONS[index]
        row_from = {-1: pl.ds(0, 1), 0: pl.ds(0, rows), 1: pl.ds(rows - 1, 1)}[a]
        row_to = {-1: pl.ds(rows + 1, 1), 0: pl.ds(1, rows), 1: pl.ds(0, 1)}[a]
        col_from = {-1: pl.ds(0, PAD), 0: pl.ds(0, cols), 1: pl.ds(cols - PAD, PAD)}[b]
        col_to = {-1: pl.ds(PAD + cols, PAD), 0: pl.ds(PAD, cols), 1: pl.ds(0, PAD)}[b]
        return pltpu.make_async_remote_copy(
            src_ref=amp.at[0, row_from, col_from, :],
            dst_ref=tile.at[row_to, col_to, :],
            send_sem=halo_send.at[index],
            recv_sem=halo_recv.at[index],
            device_id={"inline": i + a, "xline": x + b},
            device_id_type=MESH,
        )

    for index, (a, b) in enumerate(DIRECTIONS):

        @pl.when(inside(a, b))
        def _():
            halo(index).start()

    for load in loads:
        load.wait()
    dips = [lane_dips(d_il[...], rows, cols), lane_dips(d_xl[...], rows, cols)]
    lanes = rows * cols
    dips = [jnp.broadcast_to(dip, (NWIN, lanes)) for dip in dips]
    win = lax.broadcasted_iota(jnp.int32, (NWIN, lanes), 0)

    def turn(a, b):
        block = tile[1 + a : 1 + a + rows, PAD + b : PAD + b + cols, :]
        slot = OFFSETS.index((a, b))
        times[slot] = block.reshape(lanes, TIME_SAMPLES).T
        for r in range(WIN):
            taken = times[slot, pl.ds(r, NWIN, stride=WIN), :]
            rows_of[slot, PAD + r] = taken
            if r < PAD:
                later = jnp.where(win == NWIN - 1, 0.0, pltpu.roll(taken, NWIN - 1, 0))
                rows_of[slot, PAD + WIN + r] = later
            if r >= WIN - PAD:
                rows_of[slot, PAD + r - WIN] = jnp.where(win == 0, 0.0, pltpu.roll(taken, 1, 0))

    turn(0, 0)
    for index in range(len(DIRECTIONS) - 1, -1, -1):
        a, b = DIRECTIONS[index]

        @pl.when(inside(-a, -b))
        def _():
            halo(index).wait_recv()

        turn(-a, -b)

    def stack_chunk(chunk):
        first = chunk * CHUNK
        total = [None] * CHUNK
        squares = [None] * CHUNK
        for slot, (a, b) in enumerate(OFFSETS):
            reach = (abs(a) + abs(b)) * MAX_DIP_STEP
            taps = [
                rows_of[slot, first + REACH - reach + k]
                for k in range(CHUNK + 2 * reach)
            ]
            moved = taps
            if reach:
                moved = select_shift(taps, float(a) * dips[0] + float(b) * dips[1], reach)
            for k in range(CHUNK):
                square = moved[k] * moved[k]
                total[k] = moved[k] if total[k] is None else total[k] + moved[k]
                squares[k] = square if squares[k] is None else squares[k] + square
        return total, squares

    def window(values):
        twos = [values[k] + values[k + 1] for k in range(len(values) - 1)]
        fours = [twos[k] + twos[k + 2] for k in range(len(twos) - 2)]
        return [fours[k] + fours[k + 4] + values[k + 8] for k in range(CHUNK)]

    def share(chunk, other):
        return pltpu.make_async_remote_copy(
            src_ref=attr.at[pl.ds(chunk * CHUNK, CHUNK)],
            dst_ref=base.at[pl.ds(chunk * CHUNK, CHUNK)],
            send_sem=base_send.at[chunk, direct.index(other)],
            recv_sem=base_recv.at[chunk],
            device_id={"vintage": other},
            device_id_type=MESH,
        )

    def pass_on(chunk):
        return pltpu.make_async_remote_copy(
            src_ref=base.at[pl.ds(chunk * CHUNK, CHUNK)],
            dst_ref=base.at[pl.ds(chunk * CHUNK, CHUNK)],
            send_sem=base_send.at[chunk, 0],
            recv_sem=base_recv.at[chunk],
            device_id={"vintage": v + 1},
            device_id_type=MESH,
        )

    def attribute_chunk(chunk, carried):
        total, squares = stack_chunk(chunk + 1)
        first = chunk * CHUNK
        sums = list(carried[0]) + total
        numer = window([s * s for s in sums])
        denom = window(list(carried[1]) + squares)
        for k in range(CHUNK):
            semb = numer[k] / (9.0 * denom[k] + EPS)
            semb_t[pl.ds(first + k, NWIN, stride=WIN), :] = semb
            attr[first + k] = semb * sums[RT + k] * (1.0 / 9.0)

        @pl.when(v == 0)
        def _():
            for other in reversed(direct):
                share(chunk, other).start()

        return total, squares

    lax.fori_loop(0, CHUNKS, attribute_chunk, stack_chunk(0))

    semb_n[...] = semb_t[...].T

    @pl.when(v == 0)
    def _():
        base[...] = attr[...]

    def energy(ref):
        parts = [ref[k] * ref[k] for k in range(WIN)]
        while len(parts) > 1:
            parts = [parts[k] + parts[k + 1] for k in range(0, len(parts), 2)]
        return jnp.sum(parts[0], axis=0, keepdims=True)

    mon_energy = energy(attr)

    acc = [jnp.zeros((NWIN, lanes), jnp.float32)] * LAGS
    for chunk in range(CHUNKS):

        @pl.when(v != 0)
        def _():
            pass_on(chunk).wait_recv()

            @pl.when(passes_on)
            def _():
                pass_on(chunk).start()

        placed = []
        for r in range(chunk * CHUNK, (chunk + 1) * CHUNK):
            row = base[r]
            placed.append((HALF + r, row))
            if r < HALF:
                later = jnp.where(win == NWIN - 1, 0.0, pltpu.roll(row, NWIN - 1, 0))
                placed.append((HALF + WIN + r, later))
            if r >= WIN - HALF:
                earlier = jnp.where(win == 0, 0.0, pltpu.roll(row, 1, 0))
                placed.append((HALF + r - WIN, earlier))
        for lag in range(LAGS):
            for place, row in placed:
                if 0 <= place - lag < WIN:
                    acc[lag] = acc[lag] + attr[place - lag] * row

    factor = jnp.broadcast_to(NWIN / jnp.sqrt(mon_energy * energy(base) + EPS), (NWIN, lanes))
    for lag in range(LAGS):
        corr_t[lag * NWIN : (lag + 1) * NWIN, :] = acc[lag] * factor
    corr_n[:, 0:TIME_SAMPLES] = corr_t[0:TIME_SAMPLES, :].T
    corr_n[:, TIME_SAMPLES : LAGS * NWIN] = corr_t[TIME_SAMPLES : LAGS * NWIN, :].T

    for index, (a, b) in enumerate(DIRECTIONS):

        @pl.when(inside(a, b))
        def _():
            halo(index).wait_send()

    @pl.when(v == 0)
    def _():
        for chunk in range(CHUNKS):
            for other in direct:
                share(chunk, other).wait_send()

    @pl.when(passes_on)
    def _():
        for chunk in range(CHUNKS):
            pass_on(chunk).wait_send()


def store_kernel(semb_n, corr_n, semb_out, corr_out, store_sem):
    stores = [
        pltpu.make_async_copy(semb_n, semb_out, store_sem.at[0]),
        pltpu.make_async_copy(corr_n, corr_out, store_sem.at[1]),
    ]
    for store in stores:
        store.start()
    for store in stores:
        store.wait()


def per_device(vintages, inlines, xlines, amplitude, inline_slope, crossline_slope):
    _, rows, cols, _ = amplitude.shape
    lanes = rows * cols
    f32 = jnp.float32
    in_hbm = pl.BlockSpec(memory_space=pltpu.HBM)
    in_vmem = pl.BlockSpec(memory_space=pltpu.VMEM)
    operands = [
        pltpu.with_memory_space_constraint(array, pltpu.HBM)
        for array in (amplitude, inline_slope, crossline_slope)
    ]
    held = pl.pallas_call(
        functools.partial(steer_kernel, rows, cols, vintages, inlines, xlines),
        out_shape=(
            pltpu.VMEM((lanes, TIME_SAMPLES), f32),
            pltpu.VMEM((lanes, LAGS * NWIN), f32),
        ),
        in_specs=[in_hbm] * 3,
        out_specs=(in_vmem,) * 2,
        scratch_shapes=[
            pltpu.VMEM((rows + 2, cols + 2 * PAD, TIME_SAMPLES), f32),
            pltpu.VMEM((len(OFFSETS), TIME_SAMPLES, lanes), f32),
            pltpu.VMEM((len(OFFSETS), WIN + 2 * PAD, NWIN, lanes), f32),
            pltpu.VMEM((TIME_SAMPLES, lanes), f32),
            pltpu.VMEM((WIN, NWIN, lanes), f32),
            pltpu.VMEM((WIN, NWIN, lanes), f32),
            pltpu.VMEM((LAGS * NWIN, lanes), f32),
            pltpu.VMEM((rows, cols), jnp.int32),
            pltpu.VMEM((rows, cols), jnp.int32),
            pltpu.SemaphoreType.DMA((3,)),
            pltpu.SemaphoreType.DMA((len(DIRECTIONS),)),
            pltpu.SemaphoreType.DMA((len(DIRECTIONS),)),
            pltpu.SemaphoreType.DMA((CHUNKS, max(vintages // 2 + 1, 1))),
            pltpu.SemaphoreType.DMA((CHUNKS,)),
        ],
        compiler_params=pltpu.CompilerParams(
            collective_id=0, has_side_effects=True, vmem_limit_bytes=16 * 2**20
        ),
        name="steer",
    )(*operands)
    semb, correl = pl.pallas_call(
        store_kernel,
        out_shape=(
            pltpu.HBM((lanes, TIME_SAMPLES), f32),
            pltpu.HBM((lanes, LAGS * NWIN), f32),
        ),
        in_specs=[in_vmem] * 2,
        out_specs=(in_hbm, in_hbm),
        scratch_shapes=[
            pltpu.SemaphoreType.DMA((2,)),
        ],
        compiler_params=pltpu.CompilerParams(vmem_limit_bytes=16 * 2**20),
        name="store",
    )(*[pltpu.with_memory_space_constraint(array, pltpu.VMEM) for array in held])
    return (
        semb.reshape(1, rows, cols, TIME_SAMPLES),
        correl.reshape(1, rows, cols, LAGS * NWIN),
    )


def solution(mesh):
    sizes = [mesh.shape[axis] for axis in ("vintage", "inline", "xline")]
    return jax.shard_map(
        functools.partial(per_device, *sizes),
        mesh=mesh,
        in_specs=(
            P("vintage", "inline", "xline", None),
            P("vintage", "inline", "xline"),
            P("vintage", "inline", "xline"),
        ),
        out_specs=(P("vintage", "inline", "xline", None), P("vintage", "inline", "xline", None)),
        check_vma=False,
    )
```

```python
import functools

import jax
import jax.numpy as jnp
from jax import lax
from jax.experimental import pallas as pl
from jax.experimental.pallas import tpu as pltpu
from jax.sharding import PartitionSpec as P

TIME_SAMPLES = 256
MAX_DIP_STEP = 2
RT = 4
LAGS = 33
NWIN = 8
EPS = 1e-06

WIN = TIME_SAMPLES // NWIN
HALF = LAGS // 2
REACH = 2 * MAX_DIP_STEP
PAD = 8
CHUNK = 8
CHUNKS = WIN // CHUNK
MESH = pl.DeviceIdType.MESH
DIRECTIONS = [(a, b) for a in (-1, 0, 1) for b in (-1, 0, 1) if (a, b) != (0, 0)]
ARRIVALS = [(1, 0), (-1, 0), (0, 1), (0, -1), (1, 1), (1, -1), (-1, 1), (-1, -1)]
OFFSETS = [(a, b) for a in (-1, 0, 1) for b in (-1, 0, 1)]


def lane_dips(dips, rows, cols):
    lanes = rows * cols
    col = lax.broadcasted_iota(jnp.int32, (cols, lanes), 0)
    lane = lax.broadcasted_iota(jnp.int32, (cols, lanes), 1)
    spread = jnp.where(lane % cols == col, 1.0, 0.0).astype(jnp.float32)
    tiled = jnp.dot(dips.astype(jnp.float32), spread, preferred_element_type=jnp.float32)
    row = lax.broadcasted_iota(jnp.int32, (rows, lanes), 0)
    here = lax.broadcasted_iota(jnp.int32, (rows, lanes), 1) // cols == row
    return jnp.sum(jnp.where(here, tiled, 0.0), axis=0, keepdims=True)


def select_shift(rows, shift, reach):
    left = shift + float(reach)
    step = 8 if reach > 3 else 4
    while step:
        on = left >= float(step)
        left = jnp.where(on, left - float(step), left)
        count = len(rows) - step if step > 1 else CHUNK
        keep = min(count, len(rows))
        need = CHUNK + step - 1
        rows = [
            jnp.where(on, rows[k + step], rows[k]) if k + step < len(rows) else rows[k]
            for k in range(min(len(rows), need))
        ]
        step //= 2
    return rows[:CHUNK]


def steer_kernel(
    rows, cols, vintages, inlines, xlines,
    amp, dip_il, dip_xl, semb_n, corr_n,
    tile, times, rows_of, semb_t, attr, base, corr_t, d_il, d_xl,
    load_sem, halo_send, halo_recv, base_send, base_recv,
):
    v = lax.axis_index("vintage")
    i = lax.axis_index("inline")
    x = lax.axis_index("xline")
    loads = [
        pltpu.make_async_copy(amp.at[0], tile.at[pl.ds(1, rows), pl.ds(PAD, cols), :], load_sem.at[0]),
        pltpu.make_async_copy(dip_il.at[0], d_il, load_sem.at[1]),
        pltpu.make_async_copy(dip_xl.at[0], d_xl, load_sem.at[2]),
    ]
    for load in loads:
        load.start()

    edge = jnp.zeros((PAD, TIME_SAMPLES), jnp.float32)
    for row in range(rows + 2):
        tile[row, 0:PAD, :] = edge
        tile[row, PAD + cols : 2 * PAD + cols, :] = edge
    for row in (0, rows + 1):
        tile[row, PAD : PAD + cols, :] = jnp.zeros((cols, TIME_SAMPLES), jnp.float32)

    def inside(a, b):
        return (i + a >= 0) & (i + a < inlines) & (x + b >= 0) & (x + b < xlines)

    barrier = pltpu.get_barrier_semaphore()
    greeted = jnp.int32(0)
    for a, b in DIRECTIONS:
        there = inside(a, b)
        greeted = greeted + jnp.where(there, 1, 0)

        @pl.when(there)
        def _():
            pl.semaphore_signal(
                barrier, inc=1, device_id={"inline": i + a, "xline": x + b}, device_id_type=MESH
            )

    direct = [other for other in range(1, vintages) if other == 1 or other % 2 == 0]
    passes_on = (v % 2 == 0) & (v > 0) & (v + 1 < vintages)

    @pl.when(v != 0)
    def _():
        parent = jnp.where((v % 2 == 1) & (v > 1), v - 1, 0)
        pl.semaphore_signal(barrier, inc=1, device_id={"vintage": parent}, device_id_type=MESH)

    greeted = greeted + jnp.where(v == 0, len(direct), 0) + jnp.where(passes_on, 1, 0)
    pl.semaphore_wait(barrier, greeted)

    def halo(index):
        a, b = DIRECTIONS[index]
        row_from = {-1: pl.ds(0, 1), 0: pl.ds(0, rows), 1: pl.ds(rows - 1, 1)}[a]
        row_to = {-1: pl.ds(rows + 1, 1), 0: pl.ds(1, rows), 1: pl.ds(0, 1)}[a]
        col_from = {-1: pl.ds(0, PAD), 0: pl.ds(0, cols), 1: pl.ds(cols - PAD, PAD)}[b]
        col_to = {-1: pl.ds(PAD + cols, PAD), 0: pl.ds(PAD, cols), 1: pl.ds(0, PAD)}[b]
        return pltpu.make_async_remote_copy(
            src_ref=amp.at[0, row_from, col_from, :],
            dst_ref=tile.at[row_to, col_to, :],
            send_sem=halo_send.at[index],
            recv_sem=halo_recv.at[index],
            device_id={"inline": i + a, "xline": x + b},
            device_id_type=MESH,
        )

    for index, (a, b) in enumerate(DIRECTIONS):

        @pl.when(inside(a, b))
        def _():
            halo(index).start()

    for load in loads:
        load.wait()
    dips = [lane_dips(d_il[...], rows, cols), lane_dips(d_xl[...], rows, cols)]
    lanes = rows * cols
    dips = [jnp.broadcast_to(dip, (NWIN, lanes)) for dip in dips]
    win = lax.broadcasted_iota(jnp.int32, (NWIN, lanes), 0)

    def turn(a, b):
        block = tile[1 + a : 1 + a + rows, PAD + b : PAD + b + cols, :]
        slot = OFFSETS.index((a, b))
        times[slot] = block.reshape(lanes, TIME_SAMPLES).T
        for r in range(WIN):
            taken = times[slot, pl.ds(r, NWIN, stride=WIN), :]
            rows_of[slot, PAD + r] = taken
            if r < PAD:
                later = jnp.where(win == NWIN - 1, 0.0, pltpu.roll(taken, NWIN - 1, 0))
                rows_of[slot, PAD + WIN + r] = later
            if r >= WIN - PAD:
                rows_of[slot, PAD + r - WIN] = jnp.where(win == 0, 0.0, pltpu.roll(taken, 1, 0))

    turn(0, 0)
    for a, b in ARRIVALS:
        index = DIRECTIONS.index((a, b))

        @pl.when(inside(-a, -b))
        def _():
            halo(index).wait_recv()

        turn(-a, -b)

    def stack_chunk(chunk):
        first = chunk * CHUNK
        total = [None] * CHUNK
        squares = [None] * CHUNK
        for slot, (a, b) in enumerate(OFFSETS):
            reach = (abs(a) + abs(b)) * MAX_DIP_STEP
            taps = [
                rows_of[slot, first + REACH - reach + k]
                for k in range(CHUNK + 2 * reach)
            ]
            moved = taps
            if reach:
                moved = select_shift(taps, float(a) * dips[0] + float(b) * dips[1], reach)
            for k in range(CHUNK):
                square = moved[k] * moved[k]
                total[k] = moved[k] if total[k] is None else total[k] + moved[k]
                squares[k] = square if squares[k] is None else squares[k] + square
        return total, squares

    def window(values):
        twos = [values[k] + values[k + 1] for k in range(len(values) - 1)]
        fours = [twos[k] + twos[k + 2] for k in range(len(twos) - 2)]
        return [fours[k] + fours[k + 4] + values[k + 8] for k in range(CHUNK)]

    def share(chunk, other):
        return pltpu.make_async_remote_copy(
            src_ref=attr.at[pl.ds(chunk * CHUNK, CHUNK)],
            dst_ref=base.at[pl.ds(chunk * CHUNK, CHUNK)],
            send_sem=base_send.at[chunk, direct.index(other)],
            recv_sem=base_recv.at[chunk],
            device_id={"vintage": other},
            device_id_type=MESH,
        )

    def pass_on(chunk):
        return pltpu.make_async_remote_copy(
            src_ref=base.at[pl.ds(chunk * CHUNK, CHUNK)],
            dst_ref=base.at[pl.ds(chunk * CHUNK, CHUNK)],
            send_sem=base_send.at[chunk, 0],
            recv_sem=base_recv.at[chunk],
            device_id={"vintage": v + 1},
            device_id_type=MESH,
        )

    def attribute_chunk(chunk, carried):
        total, squares = stack_chunk(chunk + 1)
        first = chunk * CHUNK
        sums = list(carried[0]) + total
        numer = window([s * s for s in sums])
        denom = window(list(carried[1]) + squares)
        for k in range(CHUNK):
            semb = numer[k] / (9.0 * denom[k] + EPS)
            semb_t[pl.ds(first + k, NWIN, stride=WIN), :] = semb
            attr[first + k] = semb * sums[RT + k] * (1.0 / 9.0)

        @pl.when(v == 0)
        def _():
            for other in reversed(direct):
                share(chunk, other).start()

        return total, squares

    lax.fori_loop(0, CHUNKS, attribute_chunk, stack_chunk(0))

    semb_n[...] = semb_t[...].T

    @pl.when(v == 0)
    def _():
        base[...] = attr[...]

    def energy(ref):
        parts = [ref[k] * ref[k] for k in range(WIN)]
        while len(parts) > 1:
            parts = [parts[k] + parts[k + 1] for k in range(0, len(parts), 2)]
        return jnp.sum(parts[0], axis=0, keepdims=True)

    mon_energy = energy(attr)

    acc = [jnp.zeros((NWIN, lanes), jnp.float32)] * LAGS
    for chunk in range(CHUNKS):

        @pl.when(v != 0)
        def _():
            pass_on(chunk).wait_recv()

            @pl.when(passes_on)
            def _():
                pass_on(chunk).start()

        placed = []
        for r in range(chunk * CHUNK, (chunk + 1) * CHUNK):
            row = base[r]
            placed.append((HALF + r, row))
            if r < HALF:
                later = jnp.where(win == NWIN - 1, 0.0, pltpu.roll(row, NWIN - 1, 0))
                placed.append((HALF + WIN + r, later))
            if r >= WIN - HALF:
                earlier = jnp.where(win == 0, 0.0, pltpu.roll(row, 1, 0))
                placed.append((HALF + r - WIN, earlier))
        for lag in range(LAGS):
            for place, row in placed:
                if 0 <= place - lag < WIN:
                    acc[lag] = acc[lag] + attr[place - lag] * row

    factor = jnp.broadcast_to(NWIN / jnp.sqrt(mon_energy * energy(base) + EPS), (NWIN, lanes))
    for lag in range(LAGS):
        corr_t[lag * NWIN : (lag + 1) * NWIN, :] = acc[lag] * factor
    corr_n[:, 0:TIME_SAMPLES] = corr_t[0:TIME_SAMPLES, :].T
    corr_n[:, TIME_SAMPLES : LAGS * NWIN] = corr_t[TIME_SAMPLES : LAGS * NWIN, :].T

    for index, (a, b) in enumerate(DIRECTIONS):

        @pl.when(inside(a, b))
        def _():
            halo(index).wait_send()

    @pl.when(v == 0)
    def _():
        for chunk in range(CHUNKS):
            for other in direct:
                share(chunk, other).wait_send()

    @pl.when(passes_on)
    def _():
        for chunk in range(CHUNKS):
            pass_on(chunk).wait_send()


def store_kernel(semb_n, corr_n, semb_out, corr_out, store_sem):
    stores = [
        pltpu.make_async_copy(semb_n, semb_out, store_sem.at[0]),
        pltpu.make_async_copy(corr_n, corr_out, store_sem.at[1]),
    ]
    for store in stores:
        store.start()
    for store in stores:
        store.wait()


def per_device(vintages, inlines, xlines, amplitude, inline_slope, crossline_slope):
    _, rows, cols, _ = amplitude.shape
    lanes = rows * cols
    f32 = jnp.float32
    in_hbm = pl.BlockSpec(memory_space=pltpu.HBM)
    in_vmem = pl.BlockSpec(memory_space=pltpu.VMEM)
    operands = [
        pltpu.with_memory_space_constraint(array, pltpu.HBM)
        for array in (amplitude, inline_slope, crossline_slope)
    ]
    held = pl.pallas_call(
        functools.partial(steer_kernel, rows, cols, vintages, inlines, xlines),
        out_shape=(
            pltpu.VMEM((lanes, TIME_SAMPLES), f32),
            pltpu.VMEM((lanes, LAGS * NWIN), f32),
        ),
        in_specs=[in_hbm] * 3,
        out_specs=(in_vmem,) * 2,
        scratch_shapes=[
            pltpu.VMEM((rows + 2, cols + 2 * PAD, TIME_SAMPLES), f32),
            pltpu.VMEM((len(OFFSETS), TIME_SAMPLES, lanes), f32),
            pltpu.VMEM((len(OFFSETS), WIN + 2 * PAD, NWIN, lanes), f32),
            pltpu.VMEM((TIME_SAMPLES, lanes), f32),
            pltpu.VMEM((WIN, NWIN, lanes), f32),
            pltpu.VMEM((WIN, NWIN, lanes), f32),
            pltpu.VMEM((LAGS * NWIN, lanes), f32),
            pltpu.VMEM((rows, cols), jnp.int32),
            pltpu.VMEM((rows, cols), jnp.int32),
            pltpu.SemaphoreType.DMA((3,)),
            pltpu.SemaphoreType.DMA((len(DIRECTIONS),)),
            pltpu.SemaphoreType.DMA((len(DIRECTIONS),)),
            pltpu.SemaphoreType.DMA((CHUNKS, max(vintages // 2 + 1, 1))),
            pltpu.SemaphoreType.DMA((CHUNKS,)),
        ],
        compiler_params=pltpu.CompilerParams(
            collective_id=0, has_side_effects=True, vmem_limit_bytes=16 * 2**20
        ),
        name="steer",
    )(*operands)
    semb, correl = pl.pallas_call(
        store_kernel,
        out_shape=(
            pltpu.HBM((lanes, TIME_SAMPLES), f32),
            pltpu.HBM((lanes, LAGS * NWIN), f32),
        ),
        in_specs=[in_vmem] * 2,
        out_specs=(in_hbm, in_hbm),
        scratch_shapes=[
            pltpu.SemaphoreType.DMA((2,)),
        ],
        compiler_params=pltpu.CompilerParams(vmem_limit_bytes=16 * 2**20),
        name="store",
    )(*[pltpu.with_memory_space_constraint(array, pltpu.VMEM) for array in held])
    return (
        semb.reshape(1, rows, cols, TIME_SAMPLES),
        correl.reshape(1, rows, cols, LAGS * NWIN),
    )


def solution(mesh):
    sizes = [mesh.shape[axis] for axis in ("vintage", "inline", "xline")]
    return jax.shard_map(
        functools.partial(per_device, *sizes),
        mesh=mesh,
        in_specs=(
            P("vintage", "inline", "xline", None),
            P("vintage", "inline", "xline"),
            P("vintage", "inline", "xline"),
        ),
        out_specs=(P("vintage", "inline", "xline", None), P("vintage", "inline", "xline", None)),
        check_vma=False,
    )
```

```python
import functools

import jax
import jax.numpy as jnp
from jax import lax
from jax.experimental import pallas as pl
from jax.experimental.pallas import tpu as pltpu
from jax.sharding import PartitionSpec as P

TIME_SAMPLES = 256
MAX_DIP_STEP = 2
RT = 4
LAGS = 33
NWIN = 8
EPS = 1e-06

WIN = TIME_SAMPLES // NWIN
HALF = LAGS // 2
REACH = 2 * MAX_DIP_STEP
PAD = 8
CHUNK = 8
CHUNKS = WIN // CHUNK
MESH = pl.DeviceIdType.MESH
DIRECTIONS = [(a, b) for a in (-1, 0, 1) for b in (-1, 0, 1) if (a, b) != (0, 0)]
ARRIVALS = [(1, 0), (-1, 0), (0, 1), (0, -1), (1, 1), (1, -1), (-1, 1), (-1, -1)]
OFFSETS = [(a, b) for a in (-1, 0, 1) for b in (-1, 0, 1)]


def lane_dips(dips, rows, cols):
    lanes = rows * cols
    col = lax.broadcasted_iota(jnp.int32, (cols, lanes), 0)
    lane = lax.broadcasted_iota(jnp.int32, (cols, lanes), 1)
    spread = jnp.where(lane % cols == col, 1.0, 0.0).astype(jnp.float32)
    tiled = jnp.dot(dips.astype(jnp.float32), spread, preferred_element_type=jnp.float32)
    row = lax.broadcasted_iota(jnp.int32, (rows, lanes), 0)
    here = lax.broadcasted_iota(jnp.int32, (rows, lanes), 1) // cols == row
    return jnp.sum(jnp.where(here, tiled, 0.0), axis=0, keepdims=True)


def select_shift(rows, shift, reach):
    left = shift + float(reach)
    step = 8 if reach > 3 else 4
    while step:
        on = left >= float(step)
        left = jnp.where(on, left - float(step), left)
        count = len(rows) - step if step > 1 else CHUNK
        keep = min(count, len(rows))
        need = CHUNK + step - 1
        rows = [
            jnp.where(on, rows[k + step], rows[k]) if k + step < len(rows) else rows[k]
            for k in range(min(len(rows), need))
        ]
        step //= 2
    return rows[:CHUNK]


def steer_kernel(
    rows, cols, vintages, inlines, xlines,
    amp, dip_il, dip_xl, semb_n, corr_n,
    tile, times, rows_of, semb_t, attr, base, corr_t, d_il, d_xl,
    load_sem, halo_send, halo_recv, base_send, base_recv,
):
    v = lax.axis_index("vintage")
    i = lax.axis_index("inline")
    x = lax.axis_index("xline")
    loads = [
        pltpu.make_async_copy(amp.at[0], tile.at[pl.ds(1, rows), pl.ds(PAD, cols), :], load_sem.at[0]),
        pltpu.make_async_copy(dip_il.at[0], d_il, load_sem.at[1]),
        pltpu.make_async_copy(dip_xl.at[0], d_xl, load_sem.at[2]),
    ]
    for load in loads:
        load.start()

    edge = jnp.zeros((PAD, TIME_SAMPLES), jnp.float32)
    for row in range(rows + 2):
        tile[row, 0:PAD, :] = edge
        tile[row, PAD + cols : 2 * PAD + cols, :] = edge
    for row in (0, rows + 1):
        tile[row, PAD : PAD + cols, :] = jnp.zeros((cols, TIME_SAMPLES), jnp.float32)

    def inside(a, b):
        return (i + a >= 0) & (i + a < inlines) & (x + b >= 0) & (x + b < xlines)

    barrier = pltpu.get_barrier_semaphore()
    greeted = jnp.int32(0)
    for a, b in DIRECTIONS:
        there = inside(a, b)
        greeted = greeted + jnp.where(there, 1, 0)

        @pl.when(there)
        def _():
            pl.semaphore_signal(
                barrier, inc=1, device_id={"inline": i + a, "xline": x + b}, device_id_type=MESH
            )

    direct = [other for other in range(1, vintages) if other == 1 or other % 2 == 0]
    passes_on = (v % 2 == 0) & (v > 0) & (v + 1 < vintages)

    @pl.when(v != 0)
    def _():
        parent = jnp.where((v % 2 == 1) & (v > 1), v - 1, 0)
        pl.semaphore_signal(barrier, inc=1, device_id={"vintage": parent}, device_id_type=MESH)

    greeted = greeted + jnp.where(v == 0, len(direct), 0) + jnp.where(passes_on, 1, 0)
    pl.semaphore_wait(barrier, greeted)

    def halo(index):
        a, b = DIRECTIONS[index]
        row_from = {-1: pl.ds(0, 1), 0: pl.ds(0, rows), 1: pl.ds(rows - 1, 1)}[a]
        row_to = {-1: pl.ds(rows + 1, 1), 0: pl.ds(1, rows), 1: pl.ds(0, 1)}[a]
        col_from = {-1: pl.ds(0, PAD), 0: pl.ds(0, cols), 1: pl.ds(cols - PAD, PAD)}[b]
        col_to = {-1: pl.ds(PAD + cols, PAD), 0: pl.ds(PAD, cols), 1: pl.ds(0, PAD)}[b]
        return pltpu.make_async_remote_copy(
            src_ref=amp.at[0, row_from, col_from, :],
            dst_ref=tile.at[row_to, col_to, :],
            send_sem=halo_send.at[index],
            recv_sem=halo_recv.at[index],
            device_id={"inline": i + a, "xline": x + b},
            device_id_type=MESH,
        )

    for index, (a, b) in enumerate(DIRECTIONS):

        @pl.when(inside(a, b))
        def _():
            halo(index).start()

    for load in loads:
        load.wait()
    dips = [lane_dips(d_il[...], rows, cols), lane_dips(d_xl[...], rows, cols)]
    lanes = rows * cols
    dips = [jnp.broadcast_to(dip, (NWIN, lanes)) for dip in dips]
    win = lax.broadcasted_iota(jnp.int32, (NWIN, lanes), 0)

    def turn(a, b):
        block = tile[1 + a : 1 + a + rows, PAD + b : PAD + b + cols, :]
        slot = OFFSETS.index((a, b))
        times[slot] = block.reshape(lanes, TIME_SAMPLES).T
        for r in range(WIN):
            taken = times[slot, pl.ds(r, NWIN, stride=WIN), :]
            rows_of[slot, PAD + r] = taken
            if r < PAD:
                later = jnp.where(win == NWIN - 1, 0.0, pltpu.roll(taken, NWIN - 1, 0))
                rows_of[slot, PAD + WIN + r] = later
            if r >= WIN - PAD:
                rows_of[slot, PAD + r - WIN] = jnp.where(win == 0, 0.0, pltpu.roll(taken, 1, 0))

    turn(0, 0)
    for a, b in ARRIVALS:
        index = DIRECTIONS.index((a, b))

        @pl.when(inside(-a, -b))
        def _():
            halo(index).wait_recv()

    for a, b in ARRIVALS:
        turn(-a, -b)

    def stack_chunk(chunk):
        first = chunk * CHUNK
        total = [None] * CHUNK
        squares = [None] * CHUNK
        for slot, (a, b) in enumerate(OFFSETS):
            reach = (abs(a) + abs(b)) * MAX_DIP_STEP
            taps = [
                rows_of[slot, first + REACH - reach + k]
                for k in range(CHUNK + 2 * reach)
            ]
            moved = taps
            if reach:
                moved = select_shift(taps, float(a) * dips[0] + float(b) * dips[1], reach)
            for k in range(CHUNK):
                square = moved[k] * moved[k]
                total[k] = moved[k] if total[k] is None else total[k] + moved[k]
                squares[k] = square if squares[k] is None else squares[k] + square
        return total, squares

    def window(values):
        twos = [values[k] + values[k + 1] for k in range(len(values) - 1)]
        fours = [twos[k] + twos[k + 2] for k in range(len(twos) - 2)]
        return [fours[k] + fours[k + 4] + values[k + 8] for k in range(CHUNK)]

    def share(chunk, other):
        return pltpu.make_async_remote_copy(
            src_ref=attr.at[pl.ds(chunk * CHUNK, CHUNK)],
            dst_ref=base.at[pl.ds(chunk * CHUNK, CHUNK)],
            send_sem=base_send.at[chunk, direct.index(other)],
            recv_sem=base_recv.at[chunk],
            device_id={"vintage": other},
            device_id_type=MESH,
        )

    def pass_on(chunk):
        return pltpu.make_async_remote_copy(
            src_ref=base.at[pl.ds(chunk * CHUNK, CHUNK)],
            dst_ref=base.at[pl.ds(chunk * CHUNK, CHUNK)],
            send_sem=base_send.at[chunk, 0],
            recv_sem=base_recv.at[chunk],
            device_id={"vintage": v + 1},
            device_id_type=MESH,
        )

    def attribute_chunk(chunk, carried):
        total, squares = stack_chunk(chunk + 1)
        first = chunk * CHUNK
        sums = list(carried[0]) + total
        numer = window([s * s for s in sums])
        denom = window(list(carried[1]) + squares)
        for k in range(CHUNK):
            semb = numer[k] / (9.0 * denom[k] + EPS)
            semb_t[pl.ds(first + k, NWIN, stride=WIN), :] = semb
            attr[first + k] = semb * sums[RT + k] * (1.0 / 9.0)

        @pl.when(v == 0)
        def _():
            for other in reversed(direct):
                share(chunk, other).start()

        return total, squares

    lax.fori_loop(0, CHUNKS, attribute_chunk, stack_chunk(0))

    semb_n[...] = semb_t[...].T

    @pl.when(v == 0)
    def _():
        base[...] = attr[...]

    def energy(ref):
        parts = [ref[k] * ref[k] for k in range(WIN)]
        while len(parts) > 1:
            parts = [parts[k] + parts[k + 1] for k in range(0, len(parts), 2)]
        return jnp.sum(parts[0], axis=0, keepdims=True)

    mon_energy = energy(attr)

    acc = [jnp.zeros((NWIN, lanes), jnp.float32)] * LAGS
    for chunk in range(CHUNKS):

        @pl.when(v != 0)
        def _():
            pass_on(chunk).wait_recv()

            @pl.when(passes_on)
            def _():
                pass_on(chunk).start()

        placed = []
        for r in range(chunk * CHUNK, (chunk + 1) * CHUNK):
            row = base[r]
            placed.append((HALF + r, row))
            if r < HALF:
                later = jnp.where(win == NWIN - 1, 0.0, pltpu.roll(row, NWIN - 1, 0))
                placed.append((HALF + WIN + r, later))
            if r >= WIN - HALF:
                earlier = jnp.where(win == 0, 0.0, pltpu.roll(row, 1, 0))
                placed.append((HALF + r - WIN, earlier))
        for lag in range(LAGS):
            for place, row in placed:
                if 0 <= place - lag < WIN:
                    acc[lag] = acc[lag] + attr[place - lag] * row

    factor = jnp.broadcast_to(NWIN / jnp.sqrt(mon_energy * energy(base) + EPS), (NWIN, lanes))
    for lag in range(LAGS):
        corr_t[lag * NWIN : (lag + 1) * NWIN, :] = acc[lag] * factor
    corr_n[:, 0:TIME_SAMPLES] = corr_t[0:TIME_SAMPLES, :].T
    corr_n[:, TIME_SAMPLES : LAGS * NWIN] = corr_t[TIME_SAMPLES : LAGS * NWIN, :].T

    for index, (a, b) in enumerate(DIRECTIONS):

        @pl.when(inside(a, b))
        def _():
            halo(index).wait_send()

    @pl.when(v == 0)
    def _():
        for chunk in range(CHUNKS):
            for other in direct:
                share(chunk, other).wait_send()

    @pl.when(passes_on)
    def _():
        for chunk in range(CHUNKS):
            pass_on(chunk).wait_send()


def store_kernel(semb_n, corr_n, semb_out, corr_out, store_sem):
    stores = [
        pltpu.make_async_copy(semb_n, semb_out, store_sem.at[0]),
        pltpu.make_async_copy(corr_n, corr_out, store_sem.at[1]),
    ]
    for store in stores:
        store.start()
    for store in stores:
        store.wait()


def per_device(vintages, inlines, xlines, amplitude, inline_slope, crossline_slope):
    _, rows, cols, _ = amplitude.shape
    lanes = rows * cols
    f32 = jnp.float32
    in_hbm = pl.BlockSpec(memory_space=pltpu.HBM)
    in_vmem = pl.BlockSpec(memory_space=pltpu.VMEM)
    operands = [
        pltpu.with_memory_space_constraint(array, pltpu.HBM)
        for array in (amplitude, inline_slope, crossline_slope)
    ]
    held = pl.pallas_call(
        functools.partial(steer_kernel, rows, cols, vintages, inlines, xlines),
        out_shape=(
            pltpu.VMEM((lanes, TIME_SAMPLES), f32),
            pltpu.VMEM((lanes, LAGS * NWIN), f32),
        ),
        in_specs=[in_hbm] * 3,
        out_specs=(in_vmem,) * 2,
        scratch_shapes=[
            pltpu.VMEM((rows + 2, cols + 2 * PAD, TIME_SAMPLES), f32),
            pltpu.VMEM((len(OFFSETS), TIME_SAMPLES, lanes), f32),
            pltpu.VMEM((len(OFFSETS), WIN + 2 * PAD, NWIN, lanes), f32),
            pltpu.VMEM((TIME_SAMPLES, lanes), f32),
            pltpu.VMEM((WIN, NWIN, lanes), f32),
            pltpu.VMEM((WIN, NWIN, lanes), f32),
            pltpu.VMEM((LAGS * NWIN, lanes), f32),
            pltpu.VMEM((rows, cols), jnp.int32),
            pltpu.VMEM((rows, cols), jnp.int32),
            pltpu.SemaphoreType.DMA((3,)),
            pltpu.SemaphoreType.DMA((len(DIRECTIONS),)),
            pltpu.SemaphoreType.DMA((len(DIRECTIONS),)),
            pltpu.SemaphoreType.DMA((CHUNKS, max(vintages // 2 + 1, 1))),
            pltpu.SemaphoreType.DMA((CHUNKS,)),
        ],
        compiler_params=pltpu.CompilerParams(
            collective_id=0, has_side_effects=True, vmem_limit_bytes=16 * 2**20
        ),
        name="steer",
    )(*operands)
    semb, correl = pl.pallas_call(
        store_kernel,
        out_shape=(
            pltpu.HBM((lanes, TIME_SAMPLES), f32),
            pltpu.HBM((lanes, LAGS * NWIN), f32),
        ),
        in_specs=[in_vmem] * 2,
        out_specs=(in_hbm, in_hbm),
        scratch_shapes=[
            pltpu.SemaphoreType.DMA((2,)),
        ],
        compiler_params=pltpu.CompilerParams(vmem_limit_bytes=16 * 2**20),
        name="store",
    )(*[pltpu.with_memory_space_constraint(array, pltpu.VMEM) for array in held])
    return (
        semb.reshape(1, rows, cols, TIME_SAMPLES),
        correl.reshape(1, rows, cols, LAGS * NWIN),
    )


def solution(mesh):
    sizes = [mesh.shape[axis] for axis in ("vintage", "inline", "xline")]
    return jax.shard_map(
        functools.partial(per_device, *sizes),
        mesh=mesh,
        in_specs=(
            P("vintage", "inline", "xline", None),
            P("vintage", "inline", "xline"),
            P("vintage", "inline", "xline"),
        ),
        out_specs=(P("vintage", "inline", "xline", None), P("vintage", "inline", "xline", None)),
        check_vma=False,
    )
```

```python
import functools

import jax
import jax.numpy as jnp
from jax import lax
from jax.experimental import pallas as pl
from jax.experimental.pallas import tpu as pltpu
from jax.sharding import PartitionSpec as P

TIME_SAMPLES = 256
MAX_DIP_STEP = 2
RT = 4
LAGS = 33
NWIN = 8
EPS = 1e-06

WIN = TIME_SAMPLES // NWIN
HALF = LAGS // 2
REACH = 2 * MAX_DIP_STEP
PAD = 8
CHUNK = 8
CHUNKS = WIN // CHUNK
MESH = pl.DeviceIdType.MESH
DIRECTIONS = [(a, b) for a in (-1, 0, 1) for b in (-1, 0, 1) if (a, b) != (0, 0)]
ARRIVALS = [(1, 0), (-1, 0), (0, 1), (0, -1), (1, 1), (1, -1), (-1, 1), (-1, -1)]
OFFSETS = [(a, b) for a in (-1, 0, 1) for b in (-1, 0, 1)]


def lane_dips(dips, rows, cols):
    lanes = rows * cols
    col = lax.broadcasted_iota(jnp.int32, (cols, lanes), 0)
    lane = lax.broadcasted_iota(jnp.int32, (cols, lanes), 1)
    spread = jnp.where(lane % cols == col, 1.0, 0.0).astype(jnp.float32)
    tiled = jnp.dot(dips.astype(jnp.float32), spread, preferred_element_type=jnp.float32)
    row = lax.broadcasted_iota(jnp.int32, (rows, lanes), 0)
    here = lax.broadcasted_iota(jnp.int32, (rows, lanes), 1) // cols == row
    return jnp.sum(jnp.where(here, tiled, 0.0), axis=0, keepdims=True)


def select_shift(rows, shift, reach):
    left = shift + float(reach)
    step = 8 if reach > 3 else 4
    while step:
        on = left >= float(step)
        left = jnp.where(on, left - float(step), left)
        count = len(rows) - step if step > 1 else CHUNK
        keep = min(count, len(rows))
        need = CHUNK + step - 1
        rows = [
            jnp.where(on, rows[k + step], rows[k]) if k + step < len(rows) else rows[k]
            for k in range(min(len(rows), need))
        ]
        step //= 2
    return rows[:CHUNK]


def steer_kernel(
    rows, cols, vintages, inlines, xlines,
    amp, dip_il, dip_xl, semb_n, corr_n,
    tile, times, rows_of, semb_t, attr, base, corr_t, d_il, d_xl,
    load_sem, halo_send, halo_recv, base_send, base_recv,
):
    v = lax.axis_index("vintage")
    i = lax.axis_index("inline")
    x = lax.axis_index("xline")
    loads = [
        pltpu.make_async_copy(amp.at[0], tile.at[pl.ds(1, rows), pl.ds(PAD, cols), :], load_sem.at[0]),
        pltpu.make_async_copy(dip_il.at[0], d_il, load_sem.at[1]),
        pltpu.make_async_copy(dip_xl.at[0], d_xl, load_sem.at[2]),
    ]
    for load in loads:
        load.start()

    edge = jnp.zeros((PAD, TIME_SAMPLES), jnp.float32)
    for row in range(rows + 2):
        tile[row, 0:PAD, :] = edge
        tile[row, PAD + cols : 2 * PAD + cols, :] = edge
    for row in (0, rows + 1):
        tile[row, PAD : PAD + cols, :] = jnp.zeros((cols, TIME_SAMPLES), jnp.float32)

    def inside(a, b):
        return (i + a >= 0) & (i + a < inlines) & (x + b >= 0) & (x + b < xlines)

    barrier = pltpu.get_barrier_semaphore()
    greeted = jnp.int32(0)
    for a, b in DIRECTIONS:
        there = inside(a, b)
        greeted = greeted + jnp.where(there, 1, 0)

        @pl.when(there)
        def _():
            pl.semaphore_signal(
                barrier, inc=1, device_id={"inline": i + a, "xline": x + b}, device_id_type=MESH
            )

    direct = [other for other in range(1, vintages) if other == 1 or other % 2 == 0]
    passes_on = (v % 2 == 0) & (v > 0) & (v + 1 < vintages)

    @pl.when(v != 0)
    def _():
        parent = jnp.where((v % 2 == 1) & (v > 1), v - 1, 0)
        pl.semaphore_signal(barrier, inc=1, device_id={"vintage": parent}, device_id_type=MESH)

    greeted = greeted + jnp.where(v == 0, len(direct), 0) + jnp.where(passes_on, 1, 0)
    pl.semaphore_wait(barrier, greeted)

    def halo(index):
        a, b = DIRECTIONS[index]
        row_from = {-1: pl.ds(0, 1), 0: pl.ds(0, rows), 1: pl.ds(rows - 1, 1)}[a]
        row_to = {-1: pl.ds(rows + 1, 1), 0: pl.ds(1, rows), 1: pl.ds(0, 1)}[a]
        col_from = {-1: pl.ds(0, PAD), 0: pl.ds(0, cols), 1: pl.ds(cols - PAD, PAD)}[b]
        col_to = {-1: pl.ds(PAD + cols, PAD), 0: pl.ds(PAD, cols), 1: pl.ds(0, PAD)}[b]
        return pltpu.make_async_remote_copy(
            src_ref=amp.at[0, row_from, col_from, :],
            dst_ref=tile.at[row_to, col_to, :],
            send_sem=halo_send.at[index],
            recv_sem=halo_recv.at[index],
            device_id={"inline": i + a, "xline": x + b},
            device_id_type=MESH,
        )

    for index, (a, b) in enumerate(DIRECTIONS):

        @pl.when(inside(a, b))
        def _():
            halo(index).start()

    for load in loads:
        load.wait()
    dips = [lane_dips(d_il[...], rows, cols), lane_dips(d_xl[...], rows, cols)]
    lanes = rows * cols
    dips = [jnp.broadcast_to(dip, (NWIN, lanes)) for dip in dips]
    win = lax.broadcasted_iota(jnp.int32, (NWIN, lanes), 0)

    def turn(a, b):
        block = tile[1 + a : 1 + a + rows, PAD + b : PAD + b + cols, :]
        slot = OFFSETS.index((a, b))
        times[slot] = block.reshape(lanes, TIME_SAMPLES).T
        for r in range(WIN):
            taken = times[slot, pl.ds(r, NWIN, stride=WIN), :]
            rows_of[slot, PAD + r] = taken
            if r < PAD:
                later = jnp.where(win == NWIN - 1, 0.0, pltpu.roll(taken, NWIN - 1, 0))
                rows_of[slot, PAD + WIN + r] = later
            if r >= WIN - PAD:
                rows_of[slot, PAD + r - WIN] = jnp.where(win == 0, 0.0, pltpu.roll(taken, 1, 0))

    turn(0, 0)
    for a, b in ARRIVALS:
        index = DIRECTIONS.index((a, b))

        @pl.when(inside(-a, -b))
        def _():
            halo(index).wait_recv()

    for a, b in ARRIVALS:
        turn(-a, -b)

    def stack_chunk(chunk):
        first = chunk * CHUNK
        total = [None] * CHUNK
        squares = [None] * CHUNK
        for slot, (a, b) in enumerate(OFFSETS):
            reach = (abs(a) + abs(b)) * MAX_DIP_STEP
            taps = [
                rows_of[slot, first + REACH - reach + k]
                for k in range(CHUNK + 2 * reach)
            ]
            moved = taps
            if reach:
                moved = select_shift(taps, float(a) * dips[0] + float(b) * dips[1], reach)
            for k in range(CHUNK):
                square = moved[k] * moved[k]
                total[k] = moved[k] if total[k] is None else total[k] + moved[k]
                squares[k] = square if squares[k] is None else squares[k] + square
        return total, squares

    def window(values):
        twos = [values[k] + values[k + 1] for k in range(len(values) - 1)]
        fours = [twos[k] + twos[k + 2] for k in range(len(twos) - 2)]
        return [fours[k] + fours[k + 4] + values[k + 8] for k in range(CHUNK)]

    def share(chunk, other):
        return pltpu.make_async_remote_copy(
            src_ref=attr.at[pl.ds(chunk * CHUNK, CHUNK)],
            dst_ref=base.at[pl.ds(chunk * CHUNK, CHUNK)],
            send_sem=base_send.at[chunk, direct.index(other)],
            recv_sem=base_recv.at[chunk],
            device_id={"vintage": other},
            device_id_type=MESH,
        )

    def pass_on(chunk):
        return pltpu.make_async_remote_copy(
            src_ref=base.at[pl.ds(chunk * CHUNK, CHUNK)],
            dst_ref=base.at[pl.ds(chunk * CHUNK, CHUNK)],
            send_sem=base_send.at[chunk, 0],
            recv_sem=base_recv.at[chunk],
            device_id={"vintage": v + 1},
            device_id_type=MESH,
        )

    def attribute_chunk(chunk, carried):
        total, squares = stack_chunk(chunk + 1)
        first = chunk * CHUNK
        sums = list(carried[0]) + total
        numer = window([s * s for s in sums])
        denom = window(list(carried[1]) + squares)
        for k in range(CHUNK):
            semb = numer[k] / (9.0 * denom[k] + EPS)
            semb_t[pl.ds(first + k, NWIN, stride=WIN), :] = semb
            attr[first + k] = semb * sums[RT + k] * (1.0 / 9.0)

        @pl.when(v == 0)
        def _():
            for other in reversed(direct):
                share(chunk, other).start()

        return total, squares

    lax.fori_loop(0, CHUNKS, attribute_chunk, stack_chunk(0))

    semb_n[...] = semb_t[...].T

    @pl.when(v == 0)
    def _():
        base[...] = attr[...]

    def energy(ref):
        parts = [ref[k] * ref[k] for k in range(WIN)]
        while len(parts) > 1:
            parts = [parts[k] + parts[k + 1] for k in range(0, len(parts), 2)]
        return jnp.sum(parts[0], axis=0, keepdims=True)

    mon_energy = energy(attr)

    acc = [jnp.zeros((NWIN, lanes), jnp.float32)] * LAGS
    @pl.when(passes_on)
    def _():
        for chunk in range(CHUNKS):
            pass_on(chunk).wait_recv()
            pass_on(chunk).start()

    for chunk in range(CHUNKS):

        @pl.when((v != 0) & jnp.logical_not(passes_on))
        def _():
            pass_on(chunk).wait_recv()

        placed = []
        for r in range(chunk * CHUNK, (chunk + 1) * CHUNK):
            row = base[r]
            placed.append((HALF + r, row))
            if r < HALF:
                later = jnp.where(win == NWIN - 1, 0.0, pltpu.roll(row, NWIN - 1, 0))
                placed.append((HALF + WIN + r, later))
            if r >= WIN - HALF:
                earlier = jnp.where(win == 0, 0.0, pltpu.roll(row, 1, 0))
                placed.append((HALF + r - WIN, earlier))
        for lag in range(LAGS):
            for place, row in placed:
                if 0 <= place - lag < WIN:
                    acc[lag] = acc[lag] + attr[place - lag] * row

    factor = jnp.broadcast_to(NWIN / jnp.sqrt(mon_energy * energy(base) + EPS), (NWIN, lanes))
    for lag in range(LAGS):
        corr_t[lag * NWIN : (lag + 1) * NWIN, :] = acc[lag] * factor
    corr_n[:, 0:TIME_SAMPLES] = corr_t[0:TIME_SAMPLES, :].T
    corr_n[:, TIME_SAMPLES : LAGS * NWIN] = corr_t[TIME_SAMPLES : LAGS * NWIN, :].T

    for index, (a, b) in enumerate(DIRECTIONS):

        @pl.when(inside(a, b))
        def _():
            halo(index).wait_send()

    @pl.when(v == 0)
    def _():
        for chunk in range(CHUNKS):
            for other in direct:
                share(chunk, other).wait_send()

    @pl.when(passes_on)
    def _():
        for chunk in range(CHUNKS):
            pass_on(chunk).wait_send()


def store_kernel(semb_n, corr_n, semb_out, corr_out, store_sem):
    stores = [
        pltpu.make_async_copy(semb_n, semb_out, store_sem.at[0]),
        pltpu.make_async_copy(corr_n, corr_out, store_sem.at[1]),
    ]
    for store in stores:
        store.start()
    for store in stores:
        store.wait()


def per_device(vintages, inlines, xlines, amplitude, inline_slope, crossline_slope):
    _, rows, cols, _ = amplitude.shape
    lanes = rows * cols
    f32 = jnp.float32
    in_hbm = pl.BlockSpec(memory_space=pltpu.HBM)
    in_vmem = pl.BlockSpec(memory_space=pltpu.VMEM)
    operands = [
        pltpu.with_memory_space_constraint(array, pltpu.HBM)
        for array in (amplitude, inline_slope, crossline_slope)
    ]
    held = pl.pallas_call(
        functools.partial(steer_kernel, rows, cols, vintages, inlines, xlines),
        out_shape=(
            pltpu.VMEM((lanes, TIME_SAMPLES), f32),
            pltpu.VMEM((lanes, LAGS * NWIN), f32),
        ),
        in_specs=[in_hbm] * 3,
        out_specs=(in_vmem,) * 2,
        scratch_shapes=[
            pltpu.VMEM((rows + 2, cols + 2 * PAD, TIME_SAMPLES), f32),
            pltpu.VMEM((len(OFFSETS), TIME_SAMPLES, lanes), f32),
            pltpu.VMEM((len(OFFSETS), WIN + 2 * PAD, NWIN, lanes), f32),
            pltpu.VMEM((TIME_SAMPLES, lanes), f32),
            pltpu.VMEM((WIN, NWIN, lanes), f32),
            pltpu.VMEM((WIN, NWIN, lanes), f32),
            pltpu.VMEM((LAGS * NWIN, lanes), f32),
            pltpu.VMEM((rows, cols), jnp.int32),
            pltpu.VMEM((rows, cols), jnp.int32),
            pltpu.SemaphoreType.DMA((3,)),
            pltpu.SemaphoreType.DMA((len(DIRECTIONS),)),
            pltpu.SemaphoreType.DMA((len(DIRECTIONS),)),
            pltpu.SemaphoreType.DMA((CHUNKS, max(vintages // 2 + 1, 1))),
            pltpu.SemaphoreType.DMA((CHUNKS,)),
        ],
        compiler_params=pltpu.CompilerParams(
            collective_id=0, has_side_effects=True, vmem_limit_bytes=16 * 2**20
        ),
        name="steer",
    )(*operands)
    semb, correl = pl.pallas_call(
        store_kernel,
        out_shape=(
            pltpu.HBM((lanes, TIME_SAMPLES), f32),
            pltpu.HBM((lanes, LAGS * NWIN), f32),
        ),
        in_specs=[in_vmem] * 2,
        out_specs=(in_hbm, in_hbm),
        scratch_shapes=[
            pltpu.SemaphoreType.DMA((2,)),
        ],
        compiler_params=pltpu.CompilerParams(vmem_limit_bytes=16 * 2**20),
        name="store",
    )(*[pltpu.with_memory_space_constraint(array, pltpu.VMEM) for array in held])
    return (
        semb.reshape(1, rows, cols, TIME_SAMPLES),
        correl.reshape(1, rows, cols, LAGS * NWIN),
    )


def solution(mesh):
    sizes = [mesh.shape[axis] for axis in ("vintage", "inline", "xline")]
    return jax.shard_map(
        functools.partial(per_device, *sizes),
        mesh=mesh,
        in_specs=(
            P("vintage", "inline", "xline", None),
            P("vintage", "inline", "xline"),
            P("vintage", "inline", "xline"),
        ),
        out_specs=(P("vintage", "inline", "xline", None), P("vintage", "inline", "xline", None)),
        check_vma=False,
    )
```
